32 devices in a mesh: row: 4 (over x, core), col: 8 (over z, y).
Axes of the slice: x: 2, y: 2, z: 4, core: 2. Of those that a mesh axis runs over, the one named last changes fastest.
Arguments:
- orbitals: bfloat16 [128, 16384], P(('row', 'col')), may hold values from -0.15722656 to 0.15722656
- gradient: bfloat16 [128, 16384], P(('row', 'col')), may hold values from -6 to 6
- stored: float32 [16384, 16384], P('row', 'col'), as said below
Outputs:
- projected: bfloat16 [128, 16384], P(('row', 'col'))
The draws below stay inside these ranges and needn't reach their ends.
Inputs may be any that keep to these rules, and one draw needn't show every extreme that they name: stored is exactly symmetric: stored[i, j] equals stored[j, i].
All inputs are finite; a program needn't handle non-finite values.
Results may differ from the reference program's by a relative error of at most 0.0034.
Values may be sent and summed in bfloat16 or wider, within the bound.
A program may use at most 64 MiB of HBM per device.

```python
import math
import jax
import jax.numpy as jnp
from jax import lax

NORB = 16384
NPW = 128


def draw_stored(key, part):
    base = jax.random.normal(key, (NORB, NORB), jnp.float32)
    return (base + base.T) * 0.18


def steps_of(key, extent, cuts, smallest, largest):
    gain = 1.0
    for axis_at, blocks in cuts:
        steps = jax.random.uniform(jax.random.fold_in(jax.random.fold_in(key, 6), axis_at), (blocks,), jnp.float32, smallest / len(cuts), largest / len(cuts))
        gain = gain * jnp.repeat(jnp.exp(steps), extent[axis_at] // blocks).reshape((-1,) + (1,) * (len(extent) - 1 - axis_at))
    return gain


def gaussian(key, extent, deviation, most, cuts=(), kind=jnp.bfloat16):
    factor_of = steps_of(key, extent, cuts, -0.22, 0.18) if cuts else 1.0
    entries = jax.random.normal(key, extent, jnp.float32) * deviation * factor_of
    return jnp.minimum(jnp.maximum(entries, -most), most).astype(kind)


def setup_inputs(seed: int = 0) -> dict:
    seeds = jax.random.split(jax.random.key(seed), 4)
    return {
        "orbitals": gaussian(seeds[0], (NPW, NORB), ((NPW * NORB) ** -0.25), 0.15722656, ((0, 32),)),
        "gradient": gaussian(seeds[1], (NPW, NORB), 1.0, 6.0, ((0, 32),)),
        "stored": draw_stored(jax.random.fold_in(seeds[3], 71), 0),
    }


def reference(orbitals, gradient, stored):
    width = math.gcd(NORB, 1024)
    count = NORB // width

    def column_block(index):
        start = (index * width).astype(jnp.int32)
        orb_cols = lax.dynamic_slice_in_dim(orbitals, start, width, 1)
        grad_cols = lax.dynamic_slice_in_dim(gradient, start, width, 1)
        kept_cols = lax.dynamic_slice_in_dim(stored, start, width, 1)
        half_cols = (0.5 * jnp.dot(orbitals.T, grad_cols, preferred_element_type=jnp.float32) + 0.5 * kept_cols).astype(jnp.bfloat16)
        half_rows = (0.5 * jnp.dot(gradient.T, orb_cols, preferred_element_type=jnp.float32) + 0.5 * kept_cols).astype(jnp.bfloat16)
        correction = jnp.dot(orbitals, half_cols, preferred_element_type=jnp.float32) + jnp.dot(orbitals, half_rows, preferred_element_type=jnp.float32)
        return (grad_cols.astype(jnp.float32) - correction).astype(jnp.bfloat16)

    blocks = lax.map(column_block, jnp.arange(count, dtype=jnp.int32))
    return jnp.transpose(blocks, (1, 0, 2)).reshape(NPW, NORB)
```

```python
import functools

import jax
import jax.numpy as jnp
from jax import lax
from jax.experimental import pallas as pl
from jax.experimental.pallas import tpu as pltpu
from jax.sharding import PartitionSpec as P

MESH = pl.DeviceIdType.MESH
LANES = 128
TILE = 16
CHUNKS = 4
S_COPIES = 8


def reorder(panel, outer, inner):
    width = panel.shape[1]
    shaped = panel.reshape(outer, inner, -1, width)
    return jnp.swapaxes(shaped, 0, 1).reshape(-1, width)


def inner_product(left, right):
    return lax.dot_general(
        left, right, (((0,), (0,)), ((), ())), preferred_element_type=jnp.float32
    )


def dot(left, right):
    return jnp.dot(left, right, preferred_element_type=jnp.float32)


def general_body(orbitals, gradient, stored):
    n_row = lax.axis_size("row")
    n_col = lax.axis_size("col")
    orb_q, grad_q = (
        lax.all_to_all(orbitals, "row", split_axis=1, concat_axis=0, tiled=True),
        lax.all_to_all(gradient, "row", split_axis=1, concat_axis=0, tiled=True),
    )
    orb_q, grad_q = (
        lax.all_gather(orb_q, "col", axis=0, tiled=True),
        lax.all_gather(grad_q, "col", axis=0, tiled=True),
    )
    orb_q = reorder(orb_q, n_col, n_row)
    grad_q = reorder(grad_q, n_col, n_row)
    orb_o, grad_o = (
        lax.all_to_all(orbitals, "col", split_axis=1, concat_axis=0, tiled=True),
        lax.all_to_all(gradient, "col", split_axis=1, concat_axis=0, tiled=True),
    )
    orb_o, grad_o = (
        lax.all_gather(orb_o, "row", axis=0, tiled=True),
        lax.all_gather(grad_o, "row", axis=0, tiled=True),
    )
    half = (0.5 * inner_product(orb_q, grad_o) + 0.5 * stored).astype(jnp.bfloat16)
    half_mirror = (0.5 * inner_product(grad_q, orb_o) + 0.5 * stored).astype(jnp.bfloat16)
    share = lax.psum_scatter(
        dot(orb_q, half) + dot(orb_q, half_mirror), "row", scatter_dimension=0, tiled=True
    )
    correction = lax.all_to_all(share, "col", split_axis=0, concat_axis=1, tiled=True)
    return (gradient.astype(jnp.float32) - correction).astype(jnp.bfloat16)


def kernel(
    n_row, n_col, own, width,
    xg, s_hbm, out,
    sbuf, rowbuf, xq, gsh, acc, rbuf, xout, xbuf, ebuf, xe, ge, perm, cbuf, ab, fbuf,
    s_sem, row_send, row_recv, e_send, e_recv, g_send, g_recv,
    c_send, c_recv, ab_send, ab_recv, core_send, core_recv, x_send, x_recv, f_send, f_recv,
):
    n_dev = n_row * n_col
    n_z = n_col // 2
    groups = width // LANES
    part = n_col // CHUNKS
    deep = part * width
    r, c = lax.axis_index("row"), lax.axis_index("col")
    me = c * n_row + r
    z, y = lax.div(c, 2), lax.rem(c, 2)
    core, chip = lax.rem(r, 2), lax.div(r, 2)
    near = chip * 2 + 1 - core
    far = (1 - chip) * 2 + core
    cross = (1 - chip) * 2 + 1 - core

    def device(d):
        return {"row": lax.rem(d, n_row), "col": lax.div(d, n_row)}

    def remote(src, dst, send, recv, target):
        return pltpu.make_async_remote_copy(
            src_ref=src, dst_ref=dst, send_sem=send, recv_sem=recv,
            device_id=target, device_id_type=MESH,
        )

    depth = sbuf.shape[0] // S_COPIES

    def s_copy(i):
        rows = pl.ds(i * depth, depth)
        return pltpu.make_async_copy(s_hbm.at[rows, :], sbuf.at[rows, :], s_sem.at[i])

    def others(count, mine, body):
        @pl.loop(1, count)
        def _(i):
            body(lax.rem(mine + i, count))

    barrier = pltpu.get_barrier_semaphore()
    others(n_dev, me, lambda d: pl.semaphore_signal(
        barrier, inc=1, device_id=device(d), device_id_type=MESH))
    for i in range(S_COPIES):
        s_copy(i).start()
    pl.semaphore_wait(barrier, n_dev - 1)

    def row_copy(p, q):
        return remote(
            xg.at[pl.ds(p * n_col, n_col)], rowbuf.at[q],
            row_send.at[p], row_recv.at[q], {"row": p, "col": c},
        )

    others(n_row, r, lambda p: row_copy(p, r).start())
    rowbuf[r] = xg[pl.ds(r * n_col, n_col)]

    def e_copy(d, s):
        return remote(xg.at[d], ebuf.at[s], e_send.at[d], e_recv.at[s], device(d))

    n_out = n_dev * TILE
    at = lax.broadcasted_iota(jnp.int32, (n_out, n_out), 0)
    of = lax.broadcasted_iota(jnp.int32, (n_out, n_out), 1)
    wide = n_dev * own
    tile_row = lax.div(lax.rem(at, wide), own) * TILE + lax.div(at, wide) * own + lax.rem(at, own)
    perm[...] = jnp.where(tile_row == of, 1.0, 0.0).astype(jnp.bfloat16)
    at = lax.broadcasted_iota(jnp.int32, (n_row * TILE, n_row * TILE), 0)
    of = lax.broadcasted_iota(jnp.int32, (n_row * TILE, n_row * TILE), 1)
    tall = n_row * own
    small_row = lax.div(lax.rem(at, tall), own) * TILE + lax.div(at, tall) * own + lax.rem(at, own)
    small = jnp.where(small_row == of, 1.0, 0.0).astype(jnp.bfloat16)

    others(n_row, r, lambda q: row_copy(q, q).wait_recv())

    def shard(k, o):
        return xq.at[k, pl.ds(pl.multiple_of(o * tall, tall), tall), :]

    def g_copy(k, o, way):
        target = (c + 2, c - 2, z * 2 + 1 - y)[way]
        return remote(
            shard(k, o), shard(k, o), g_send.at[k, o, way], g_recv.at[k, o],
            {"row": r, "col": target},
        )

    def pass_on(k, o, do, up, down):
        if up:
            pl.when(z < n_z - 1)(lambda: do(g_copy(k, o, 0)))
        if down:
            pl.when(z > 0)(lambda: do(g_copy(k, o, 1)))
        do(g_copy(k, o, 2))

    def start(copy):
        copy.start()

    def wait_send(copy):
        copy.wait_send()

    def post(k):
        mine = pl.ds(pl.multiple_of(c * tall, tall), tall)
        for b in range(part):
            for t in range(2):
                block = rowbuf[:, k * part + b, t].reshape(n_row * TILE, LANES)
                turned = dot(small, block).astype(jnp.bfloat16)
                for g in range(groups):
                    piece = turned[g * tall:(g + 1) * tall]
                    lanes = pl.ds(b * width + g * LANES, LANES)
                    gsh[k, t * tall:(t + 1) * tall, lanes] = piece
                    if t == 0:
                        xq[k, mine, lanes] = piece
        pass_on(k, c, start, True, True)

    def forward(k, d):
        @pl.when(z >= d)
        def _():
            o = c - 2 * d
            g_copy(k, o, 2).wait_recv()
            pass_on(k, o, start, True, False)

        @pl.when(z + d < n_z)
        def _():
            o = c + 2 * d
            g_copy(k, o, 2).wait_recv()
            pass_on(k, o, start, False, True)

    def blocks_product(k, j):
        rows = pl.ds(k * deep, deep)
        cols = pl.ds(pl.multiple_of(j * width, width), width)
        return dot(xq[k], sbuf[rows, cols].astype(jnp.bfloat16))

    def inner(k):
        return lax.dot_general(
            gsh[k], xq[k], (((1,), (1,)), ((), ())), preferred_element_type=jnp.float32)

    def complete(k):
        for z0 in range(n_z):
            g_copy(k, z0 * 2 + 1 - y, 2).wait_recv()
        for i in range(k * S_COPIES // CHUNKS, (k + 1) * S_COPIES // CHUNKS):
            s_copy(i).wait()

    for k in range(CHUNKS):
        post(k)
    others(n_dev, me, lambda d: e_copy(d, me).start())
    ebuf[me] = xg[me]

    gram = None
    for step in range(1, CHUNKS + n_z - 1):
        for d in range(n_z - 1, 0, -1):
            if 0 <= step - d < CHUNKS:
                forward(step - d, d)
        k = step - (n_z - 1)
        if 0 <= k < CHUNKS - 1:
            complete(k)
            gram = inner(k) if gram is None else gram + inner(k)

            @pl.loop(0, n_row)
            def _(j, k=k):
                if k == 0:
                    acc[j] = blocks_product(k, j)
                else:
                    acc[j] += blocks_product(k, j)

    last = CHUNKS - 1
    complete(last)
    cbuf[r] = gram + inner(last)

    def c_copy(p, q):
        return remote(cbuf.at[q], cbuf.at[q], c_send.at[p], c_recv.at[q], {"row": p, "col": c})

    others(n_row, r, lambda p: c_copy(p, r).start())

    def core_copy(i, j):
        return remote(acc.at[j], rbuf.at[i], core_send.at[i], core_recv.at[i],
                      {"row": near, "col": c})

    acc[cross] += blocks_product(last, cross)
    core_copy(0, cross).start()
    acc[near] += blocks_product(last, near)
    core_copy(1, near).start()

    others(n_row, r, lambda q: c_copy(q, q).wait_recv())
    total = cbuf[0]
    for q in range(1, n_row):
        total = total + cbuf[q]
    ab[c] = total

    def ab_copy(p, q):
        return remote(ab.at[q], ab.at[q], ab_send.at[p], ab_recv.at[q], {"row": r, "col": p})

    others(n_col, c, lambda p: ab_copy(p, c).start())

    acc[far] += blocks_product(last, far)
    core_copy(0, cross).wait_recv()
    xout[...] = (acc[far] + rbuf[0]).astype(jnp.bfloat16)
    x_copy = remote(xout, xbuf, x_send, x_recv, {"row": far, "col": c})
    x_copy.start()
    acc[r] += blocks_product(last, r)

    others(n_dev, me, lambda s: e_copy(s, s).wait_recv())
    for t, dest in ((0, xe), (1, ge)):
        turned = dot(perm[...], ebuf[:, t].reshape(n_out, LANES)).astype(jnp.bfloat16)
        for g in range(groups):
            dest[:, g * LANES:(g + 1) * LANES] = turned[g * wide:(g + 1) * wide]

    others(n_col, c, lambda q: ab_copy(q, q).wait_recv())
    orb_orb = ab[:, :tall, :].reshape(wide, wide)
    orb_grad = ab[:, tall:, :].reshape(wide, wide).T

    def accurate(left, right):
        high = left.astype(jnp.bfloat16)
        low = (left - high.astype(jnp.float32)).astype(jnp.bfloat16)
        return dot(high, right) + dot(low, right)

    rest = ge[...].astype(jnp.float32) - 0.5 * (
        accurate(orb_orb, ge[...]) + accurate(orb_grad, xe[...]))
    core_copy(1, near).wait_recv()
    rest = rest - (acc[r] + rbuf[1])
    x_copy.wait_recv()
    result = (rest - xbuf[...].astype(jnp.float32)).astype(jnp.bfloat16)
    stack = jnp.concatenate([result[:, g * LANES:(g + 1) * LANES] for g in range(groups)], axis=0)
    tiles = lax.dot_general(
        perm[...], stack, (((0,), (0,)), ((), ())), preferred_element_type=jnp.float32)
    fbuf[...] = tiles.astype(jnp.bfloat16).reshape(n_dev, TILE, LANES)

    def f_copy(d, s):
        return remote(fbuf.at[d], out.at[s], f_send.at[d], f_recv.at[s], device(d))

    others(n_dev, me, lambda d: f_copy(d, me).start())
    out[me] = fbuf[me]

    others(n_row, r, lambda p: row_copy(p, r).wait_send())
    others(n_row, r, lambda p: c_copy(p, r).wait_send())
    others(n_col, c, lambda p: ab_copy(p, c).wait_send())
    others(n_dev, me, lambda d: e_copy(d, me).wait_send())
    for k in range(CHUNKS):
        pass_on(k, c, wait_send, True, True)
        for d in range(1, n_z):
            pl.when(z >= d)(lambda k=k, d=d: pass_on(k, c - 2 * d, wait_send, True, False))
            pl.when(z + d < n_z)(lambda k=k, d=d: pass_on(k, c + 2 * d, wait_send, False, True))
    core_copy(0, cross).wait_send()
    core_copy(1, near).wait_send()
    x_copy.wait_send()
    others(n_dev, me, lambda s: f_copy(s, s).wait_recv())
    others(n_dev, me, lambda d: f_copy(d, me).wait_send())


def kernel_body(n_row, n_col, orbitals, gradient, stored):
    own, n_orb = orbitals.shape
    n_dev = n_row * n_col
    width = n_orb // n_dev
    groups = width // LANES
    n_pw = own * n_dev
    tall = n_row * own
    deep = n_orb // n_row // CHUNKS

    def tiled(rows):
        shaped = rows.reshape(own, n_dev, groups, LANES)
        return shaped.transpose(1, 2, 0, 3).reshape(n_dev, 1, TILE, LANES)

    xg = jnp.concatenate([tiled(orbitals), tiled(gradient)], axis=1)
    bf16, f32 = jnp.bfloat16, jnp.float32
    dma = pltpu.SemaphoreType.DMA
    tiles = pl.pallas_call(
        functools.partial(kernel, n_row, n_col, own, width),
        out_shape=jax.ShapeDtypeStruct((n_dev, TILE, LANES), bf16),
        in_specs=[pl.BlockSpec(memory_space=pltpu.VMEM), pl.BlockSpec(memory_space=pl.ANY)],
        out_specs=pl.BlockSpec(memory_space=pltpu.VMEM),
        scratch_shapes=[
            pltpu.VMEM(stored.shape, f32),
            pltpu.VMEM((n_row, n_col, 2, TILE, LANES), bf16),
            pltpu.VMEM((CHUNKS, n_pw, deep), bf16),
            pltpu.VMEM((CHUNKS, 2 * tall, deep), bf16),
            pltpu.VMEM((n_row, n_pw, width), f32),
            pltpu.VMEM((2, n_pw, width), f32),
            pltpu.VMEM((n_pw, width), bf16),
            pltpu.VMEM((n_pw, width), bf16),
            pltpu.VMEM((n_dev, 2, TILE, LANES), bf16),
            pltpu.VMEM((n_pw, width), bf16),
            pltpu.VMEM((n_pw, width), bf16),
            pltpu.VMEM((n_dev * TILE, n_dev * TILE), bf16),
            pltpu.VMEM((n_row, 2 * tall, n_pw), f32),
            pltpu.VMEM((n_col, 2 * tall, n_pw), f32),
            pltpu.VMEM((n_dev, TILE, LANES), bf16),
            dma((S_COPIES,)), dma((n_row,)), dma((n_row,)), dma((n_dev,)), dma((n_dev,)),
            dma((CHUNKS, n_col, 3)), dma((CHUNKS, n_col)),
            dma((n_row,)), dma((n_row,)), dma((n_col,)), dma((n_col,)),
            dma((2,)), dma((2,)), dma(()), dma(()), dma((n_dev,)), dma((n_dev,)),
        ],
        compiler_params=pltpu.CompilerParams(
            collective_id=0, has_side_effects=True, vmem_limit_bytes=56 * 1024 * 1024),
        cost_estimate=pl.CostEstimate(
            flops=2 * n_pw * stored.size, bytes_accessed=4 * stored.size, transcendentals=0),
    )(xg, stored)
    shaped = tiles.reshape(n_dev, groups, own, LANES)
    return shaped.transpose(2, 0, 1, 3).reshape(own, n_orb)


def body(orbitals, gradient, stored):
    n_row = lax.axis_size("row")
    n_col = lax.axis_size("col")
    own, n_orb = orbitals.shape
    n_dev = n_row * n_col
    width = n_orb // n_dev
    fits = (
        n_row == 4 and n_col % CHUNKS == 0 and width % LANES == 0
        and own * width == TILE * LANES and own * n_row == TILE
        and own * n_dev == LANES and stored.shape[0] % S_COPIES == 0
        and stored.size * 4 <= 32 * 1024 * 1024
    )
    if fits:
        return kernel_body(n_row, n_col, orbitals, gradient, stored)
    return general_body(orbitals, gradient, stored)


def solution(mesh):
    return jax.shard_map(
        body,
        mesh=mesh,
        in_specs=(P(("row", "col"), None), P(("row", "col"), None), P("row", "col")),
        out_specs=P(("row", "col"), None),
        check_vma=False,
    )
```

```python
import functools

import jax
import jax.numpy as jnp
import numpy as np
from jax import lax
from jax.experimental import pallas as pl
from jax.experimental.pallas import tpu as pltpu
from jax.sharding import PartitionSpec as P

MESH = pl.DeviceIdType.MESH
LANES = 128
TILE = 16
CHUNKS = 4
S_COPIES = 8
S_SLOTS = 6


def reorder(panel, outer, inner):
    width = panel.shape[1]
    shaped = panel.reshape(outer, inner, -1, width)
    return jnp.swapaxes(shaped, 0, 1).reshape(-1, width)


def inner_product(left, right):
    return lax.dot_general(
        left, right, (((0,), (0,)), ((), ())), preferred_element_type=jnp.float32
    )


def dot(left, right):
    return jnp.dot(left, right, preferred_element_type=jnp.float32)


def general_body(orbitals, gradient, stored):
    n_row = lax.axis_size("row")
    n_col = lax.axis_size("col")
    orb_q, grad_q = (
        lax.all_to_all(orbitals, "row", split_axis=1, concat_axis=0, tiled=True),
        lax.all_to_all(gradient, "row", split_axis=1, concat_axis=0, tiled=True),
    )
    orb_q, grad_q = (
        lax.all_gather(orb_q, "col", axis=0, tiled=True),
        lax.all_gather(grad_q, "col", axis=0, tiled=True),
    )
    orb_q = reorder(orb_q, n_col, n_row)
    grad_q = reorder(grad_q, n_col, n_row)
    orb_o, grad_o = (
        lax.all_to_all(orbitals, "col", split_axis=1, concat_axis=0, tiled=True),
        lax.all_to_all(gradient, "col", split_axis=1, concat_axis=0, tiled=True),
    )
    orb_o, grad_o = (
        lax.all_gather(orb_o, "row", axis=0, tiled=True),
        lax.all_gather(grad_o, "row", axis=0, tiled=True),
    )
    half = (0.5 * inner_product(orb_q, grad_o) + 0.5 * stored).astype(jnp.bfloat16)
    half_mirror = (0.5 * inner_product(grad_q, orb_o) + 0.5 * stored).astype(jnp.bfloat16)
    share = lax.psum_scatter(
        dot(orb_q, half) + dot(orb_q, half_mirror), "row", scatter_dimension=0, tiled=True
    )
    correction = lax.all_to_all(share, "col", split_axis=0, concat_axis=1, tiled=True)
    return (gradient.astype(jnp.float32) - correction).astype(jnp.bfloat16)


def kernel(
    n_row, n_col, own, width,
    x_hbm, g_hbm, perm_hbm, small_hbm, s_hbm, out,
    xg, small, sbuf, sb, rowbuf, xq, gsh, acc, rbuf, xout, xbuf, ebuf, xe, ge, perm, cbuf, ab, fbuf,
    in_sem, s_sem, row_send, row_recv, e_send, e_recv, g_send, g_recv,
    c_send, c_recv, ab_send, ab_recv, core_send, core_recv, x_send, x_recv, f_send, f_recv,
):
    n_dev = n_row * n_col
    n_z = n_col // 2
    groups = width // LANES
    part = n_col // CHUNKS
    deep = part * width
    r, c = lax.axis_index("row"), lax.axis_index("col")
    me = c * n_row + r
    z, y = lax.div(c, 2), lax.rem(c, 2)
    core, chip = lax.rem(r, 2), lax.div(r, 2)
    near = chip * 2 + 1 - core
    far = (1 - chip) * 2 + core
    cross = (1 - chip) * 2 + 1 - core

    def device(d):
        return {"row": lax.rem(d, n_row), "col": lax.div(d, n_row)}

    def remote(src, dst, send, recv, target):
        return pltpu.make_async_remote_copy(
            src_ref=src, dst_ref=dst, send_sem=send, recv_sem=recv,
            device_id=target, device_id_type=MESH,
        )

    depth = sbuf.shape[1]
    strip = 32

    def s_copy(i):
        return pltpu.make_async_copy(
            s_hbm.at[pl.ds(i * depth, depth), :], sbuf.at[i % S_SLOTS], s_sem.at[i])

    def convert(i):
        s_copy(i).wait()

        @pl.loop(0, depth // strip)
        def _(n):
            rows = pl.ds(pl.multiple_of(n * strip, strip), strip)
            into = pl.ds(pl.multiple_of(i * depth + n * strip, strip), strip)
            sb[into, :] = sbuf[i % S_SLOTS, rows, :].astype(jnp.bfloat16)

        if i + S_SLOTS < S_COPIES:
            s_copy(i + S_SLOTS).start()

    local = [
        pltpu.make_async_copy(x_hbm, xg.at[:, 0], in_sem.at[0]),
        pltpu.make_async_copy(g_hbm, xg.at[:, 1], in_sem.at[1]),
        pltpu.make_async_copy(small_hbm, small, in_sem.at[2]),
    ] + [
        pltpu.make_async_copy(
            perm_hbm.at[g], perm.at[:, pl.ds(g * LANES, LANES)], in_sem.at[3 + g])
        for g in range(perm_hbm.shape[0])
    ]
    for copy in local:
        copy.start()
    for i in range(S_SLOTS):
        s_copy(i).start()

    def others(count, mine, body):
        @pl.loop(1, count)
        def _(i):
            body(lax.rem(mine + i, count))

    barrier = pltpu.get_barrier_semaphore()
    others(n_dev, me, lambda d: pl.semaphore_signal(
        barrier, inc=1, device_id=device(d), device_id_type=MESH))
    for copy in local:
        copy.wait()
    pl.semaphore_wait(barrier, n_dev - 1)

    def row_copy(p, q):
        return remote(
            xg.at[pl.ds(p * n_col, n_col)], rowbuf.at[q],
            row_send.at[p], row_recv.at[q], {"row": p, "col": c},
        )

    others(n_row, r, lambda p: row_copy(p, r).start())
    rowbuf[r] = xg[pl.ds(r * n_col, n_col)]

    def e_copy(d, s):
        return remote(xg.at[d], ebuf.at[s], e_send.at[d], e_recv.at[s], device(d))

    others(n_dev, me, lambda d: e_copy(d, me).start())
    ebuf[me] = xg[me]
    n_out = n_dev * TILE
    wide = n_dev * own
    tall = n_row * own
    for i in range(S_COPIES // 2):
        convert(i)

    others(n_row, r, lambda q: row_copy(q, q).wait_recv())

    def shard(k, o):
        return xq.at[k, pl.ds(pl.multiple_of(o * tall, tall), tall), :]

    def g_copy(k, o, send, target):
        return remote(
            shard(k, o), shard(k, o), send, g_recv.at[k, o], {"row": r, "col": target})

    def along_z(k, side, d):
        return g_copy(k, c, g_send.at[k, side, d, 0], c + 2 * d if side == 0 else c - 2 * d)

    def along_y(k, side, d, o):
        return g_copy(k, o, g_send.at[k, side, d, 1], z * 2 + 1 - y)

    def spread(k, do):
        do(along_y(k, 0, 0, c))
        for d in range(1, n_z):
            pl.when(z + d < n_z)(lambda d=d: do(along_z(k, 0, d)))
            pl.when(z >= d)(lambda d=d: do(along_z(k, 1, d)))

    def start(copy):
        copy.start()

    def wait_send(copy):
        copy.wait_send()

    def post(k):
        mine = pl.ds(pl.multiple_of(c * tall, tall), tall)
        for b in range(part):
            for t in range(2):
                block = rowbuf[:, k * part + b, t].reshape(n_row * TILE, LANES)
                turned = dot(small[...], block).astype(jnp.bfloat16)
                for g in range(groups):
                    piece = turned[g * tall:(g + 1) * tall]
                    lanes = pl.ds(b * width + g * LANES, LANES)
                    gsh[k, t * tall:(t + 1) * tall, lanes] = piece
                    if t == 0:
                        xq[k, mine, lanes] = piece
        spread(k, start)

    def forward(k, do, receive):
        def step(side, d, o):
            copy = along_y(k, side, d, o)
            if receive:
                copy.wait_recv()
            do(copy)

        for d in range(1, n_z):
            pl.when(z + d < n_z)(lambda d=d: step(0, d, c + 2 * d))
            pl.when(z >= d)(lambda d=d: step(1, d, c - 2 * d))

    def blocks_product(k, j):
        rows = pl.ds(k * deep, deep)
        cols = pl.ds(pl.multiple_of(j * width, width), width)
        return dot(xq[k], sb[rows, cols])

    def inner(k):
        return lax.dot_general(
            gsh[k], xq[k], (((1,), (1,)), ((), ())), preferred_element_type=jnp.float32)

    def complete(k):
        for z0 in range(n_z):
            o = z0 * 2 + 1 - y
            along_y(k, 0, 0, o).wait_recv()

    def product(k):
        @pl.loop(0, n_row)
        def _(j):
            if k == 0:
                acc[j] = blocks_product(k, j)
            else:
                acc[j] += blocks_product(k, j)

    for k in range(CHUNKS):
        post(k)
    gram = None
    for k in range(CHUNKS + 1):
        if k < CHUNKS:
            forward(k, start, True)
        piece = S_COPIES // 2 + k
        if piece < S_COPIES:
            convert(piece)
        if 1 <= k < CHUNKS:
            complete(k - 1)
            gram = inner(k - 1) if gram is None else gram + inner(k - 1)
            product(k - 1)

    last = CHUNKS - 1
    complete(last)
    cbuf[r] = gram + inner(last)

    def c_copy(p, q):
        return remote(cbuf.at[q], cbuf.at[q], c_send.at[p], c_recv.at[q], {"row": p, "col": c})

    others(n_row, r, lambda p: c_copy(p, r).start())

    def core_copy(i, j):
        return remote(acc.at[j], rbuf.at[i], core_send.at[i], core_recv.at[i],
                      {"row": near, "col": c})

    acc[cross] += blocks_product(last, cross)
    core_copy(0, cross).start()
    acc[near] += blocks_product(last, near)
    core_copy(1, near).start()

    others(n_row, r, lambda q: c_copy(q, q).wait_recv())
    total = cbuf[0]
    for q in range(1, n_row):
        total = total + cbuf[q]
    ab[c] = total

    def ab_copy(p, q):
        return remote(ab.at[q], ab.at[q], ab_send.at[p], ab_recv.at[q], {"row": r, "col": p})

    others(n_col, c, lambda p: ab_copy(p, c).start())

    acc[far] += blocks_product(last, far)
    core_copy(0, cross).wait_recv()
    xout[...] = (acc[far] + rbuf[0]).astype(jnp.bfloat16)
    x_copy = remote(xout, xbuf, x_send, x_recv, {"row": far, "col": c})
    x_copy.start()
    acc[r] += blocks_product(last, r)

    others(n_dev, me, lambda s: e_copy(s, s).wait_recv())
    for t, dest in ((0, xe), (1, ge)):
        turned = dot(perm[...], ebuf[:, t].reshape(n_out, LANES)).astype(jnp.bfloat16)
        for g in range(groups):
            dest[:, g * LANES:(g + 1) * LANES] = turned[g * wide:(g + 1) * wide]

    others(n_col, c, lambda q: ab_copy(q, q).wait_recv())
    orb_orb = ab[:, :tall, :].reshape(wide, wide)
    orb_grad = ab[:, tall:, :].reshape(wide, wide).T

    def accurate(left, right):
        high = left.astype(jnp.bfloat16)
        low = (left - high.astype(jnp.float32)).astype(jnp.bfloat16)
        return dot(high, right) + dot(low, right)

    rest = ge[...].astype(jnp.float32) - 0.5 * (
        accurate(orb_orb, ge[...]) + accurate(orb_grad, xe[...]))
    core_copy(1, near).wait_recv()
    rest = rest - (acc[r] + rbuf[1])
    x_copy.wait_recv()
    result = (rest - xbuf[...].astype(jnp.float32)).astype(jnp.bfloat16)
    stack = jnp.concatenate([result[:, g * LANES:(g + 1) * LANES] for g in range(groups)], axis=0)
    tiles = lax.dot_general(
        perm[...], stack, (((0,), (0,)), ((), ())), preferred_element_type=jnp.float32)
    fbuf[...] = tiles.astype(jnp.bfloat16).reshape(n_dev, TILE, LANES)

    def f_copy(d, s):
        return remote(fbuf.at[d], out.at[s], f_send.at[d], f_recv.at[s], device(d))

    others(n_dev, me, lambda d: f_copy(d, me).start())
    out[me] = fbuf[me]

    others(n_row, r, lambda p: row_copy(p, r).wait_send())
    others(n_row, r, lambda p: c_copy(p, r).wait_send())
    others(n_col, c, lambda p: ab_copy(p, c).wait_send())
    others(n_dev, me, lambda d: e_copy(d, me).wait_send())
    for k in range(CHUNKS):
        spread(k, wait_send)
        forward(k, wait_send, False)
    core_copy(0, cross).wait_send()
    core_copy(1, near).wait_send()
    x_copy.wait_send()
    others(n_dev, me, lambda s: f_copy(s, s).wait_recv())
    others(n_dev, me, lambda d: f_copy(d, me).wait_send())


def kernel_body(n_row, n_col, orbitals, gradient, stored):
    own, n_orb = orbitals.shape
    n_dev = n_row * n_col
    width = n_orb // n_dev
    groups = width // LANES
    n_pw = own * n_dev
    tall = n_row * own
    deep = n_orb // n_row // CHUNKS

    def tiled(rows):
        shaped = rows.reshape(own, n_dev, groups, LANES)
        return shaped.transpose(1, 2, 0, 3).reshape(n_dev, TILE, LANES)

    def gather_rows(blocks, rows):
        perm = np.zeros((blocks * TILE, blocks * TILE), np.float32)
        for at in range(blocks * TILE):
            group, rest = divmod(at, blocks * rows)
            block, row = divmod(rest, rows)
            perm[at, block * TILE + group * rows + row] = 1.0
        if perm.shape[1] > LANES:
            perm = perm.reshape(perm.shape[0], -1, LANES).transpose(1, 0, 2)
        return jnp.asarray(perm, jnp.bfloat16)

    bf16, f32 = jnp.bfloat16, jnp.float32
    dma = pltpu.SemaphoreType.DMA
    tiles = pl.pallas_call(
        functools.partial(kernel, n_row, n_col, own, width),
        out_shape=jax.ShapeDtypeStruct((n_dev, TILE, LANES), bf16),
        in_specs=[pl.BlockSpec(memory_space=pl.ANY)] * 5,
        out_specs=pl.BlockSpec(memory_space=pltpu.VMEM),
        scratch_shapes=[
            pltpu.VMEM((n_dev, 2, TILE, LANES), bf16),
            pltpu.VMEM((n_row * TILE, n_row * TILE), bf16),
            pltpu.VMEM((S_SLOTS, stored.shape[0] // S_COPIES, stored.shape[1]), f32),
            pltpu.VMEM(stored.shape, bf16),
            pltpu.VMEM((n_row, n_col, 2, TILE, LANES), bf16),
            pltpu.VMEM((CHUNKS, n_pw, deep), bf16),
            pltpu.VMEM((CHUNKS, 2 * tall, deep), bf16),
            pltpu.VMEM((n_row, n_pw, width), f32),
            pltpu.VMEM((2, n_pw, width), f32),
            pltpu.VMEM((n_pw, width), bf16),
            pltpu.VMEM((n_pw, width), bf16),
            pltpu.VMEM((n_dev, 2, TILE, LANES), bf16),
            pltpu.VMEM((n_pw, width), bf16),
            pltpu.VMEM((n_pw, width), bf16),
            pltpu.VMEM((n_dev * TILE, n_dev * TILE), bf16),
            pltpu.VMEM((n_row, 2 * tall, n_pw), f32),
            pltpu.VMEM((n_col, 2 * tall, n_pw), f32),
            pltpu.VMEM((n_dev, TILE, LANES), bf16),
            dma((3 + n_dev * TILE // LANES,)), dma((S_COPIES,)), dma((n_row,)), dma((n_row,)), dma((n_dev,)), dma((n_dev,)),
            dma((CHUNKS, 2, n_col // 2, 2)), dma((CHUNKS, n_col)),
            dma((n_row,)), dma((n_row,)), dma((n_col,)), dma((n_col,)),
            dma((2,)), dma((2,)), dma(()), dma(()), dma((n_dev,)), dma((n_dev,)),
        ],
        compiler_params=pltpu.CompilerParams(
            collective_id=0, has_side_effects=True, vmem_limit_bytes=56 * 1024 * 1024),
        cost_estimate=pl.CostEstimate(
            flops=2 * n_pw * stored.size, bytes_accessed=4 * stored.size, transcendentals=0),
    )(tiled(orbitals), tiled(gradient), gather_rows(n_dev, own), gather_rows(n_row, own), stored)
    shaped = tiles.reshape(n_dev, groups, own, LANES)
    return shaped.transpose(2, 0, 1, 3).reshape(own, n_orb)


def body(orbitals, gradient, stored):
    n_row = lax.axis_size("row")
    n_col = lax.axis_size("col")
    own, n_orb = orbitals.shape
    n_dev = n_row * n_col
    width = n_orb // n_dev
    fits = (
        n_row == 4 and n_col % CHUNKS == 0 and width % LANES == 0
        and own * width == TILE * LANES and own * n_row == TILE
        and own * n_dev == LANES and stored.shape[0] % S_COPIES == 0
        and stored.size * 4 <= 32 * 1024 * 1024
    )
    if fits:
        return kernel_body(n_row, n_col, orbitals, gradient, stored)
    return general_body(orbitals, gradient, stored)


def solution(mesh):
    return jax.shard_map(
        body,
        mesh=mesh,
        in_specs=(P(("row", "col"), None), P(("row", "col"), None), P("row", "col")),
        out_specs=P(("row", "col"), None),
        check_vma=False,
    )
```

```python
import functools

import jax
import jax.numpy as jnp
import numpy as np
from jax import lax
from jax.experimental import pallas as pl
from jax.experimental.pallas import tpu as pltpu
from jax.sharding import PartitionSpec as P

MESH = pl.DeviceIdType.MESH
LANES = 128
TILE = 16
CHUNKS = 4
S_COPIES = 8
S_SLOTS = 6


def reorder(panel, outer, inner):
    width = panel.shape[1]
    shaped = panel.reshape(outer, inner, -1, width)
    return jnp.swapaxes(shaped, 0, 1).reshape(-1, width)


def inner_product(left, right):
    return lax.dot_general(
        left, right, (((0,), (0,)), ((), ())), preferred_element_type=jnp.float32
    )


def dot(left, right):
    return jnp.dot(left, right, preferred_element_type=jnp.float32)


def general_body(orbitals, gradient, stored):
    n_row = lax.axis_size("row")
    n_col = lax.axis_size("col")
    orb_q, grad_q = (
        lax.all_to_all(orbitals, "row", split_axis=1, concat_axis=0, tiled=True),
        lax.all_to_all(gradient, "row", split_axis=1, concat_axis=0, tiled=True),
    )
    orb_q, grad_q = (
        lax.all_gather(orb_q, "col", axis=0, tiled=True),
        lax.all_gather(grad_q, "col", axis=0, tiled=True),
    )
    orb_q = reorder(orb_q, n_col, n_row)
    grad_q = reorder(grad_q, n_col, n_row)
    orb_o, grad_o = (
        lax.all_to_all(orbitals, "col", split_axis=1, concat_axis=0, tiled=True),
        lax.all_to_all(gradient, "col", split_axis=1, concat_axis=0, tiled=True),
    )
    orb_o, grad_o = (
        lax.all_gather(orb_o, "row", axis=0, tiled=True),
        lax.all_gather(grad_o, "row", axis=0, tiled=True),
    )
    half = (0.5 * inner_product(orb_q, grad_o) + 0.5 * stored).astype(jnp.bfloat16)
    half_mirror = (0.5 * inner_product(grad_q, orb_o) + 0.5 * stored).astype(jnp.bfloat16)
    share = lax.psum_scatter(
        dot(orb_q, half) + dot(orb_q, half_mirror), "row", scatter_dimension=0, tiled=True
    )
    correction = lax.all_to_all(share, "col", split_axis=0, concat_axis=1, tiled=True)
    return (gradient.astype(jnp.float32) - correction).astype(jnp.bfloat16)


def kernel(
    n_row, n_col, own, width,
    x_hbm, g_hbm, perm_hbm, small_hbm, s_hbm, out,
    xin, gin, small, sbuf, sb, xt, grow, gblk, gt, xq, gsh, acc, rbuf, xout, xbuf, xe, ge, perm,
    cbuf, ab, fbuf, fmid,
    in_sem, s_sem, row_send, row_recv, e_send, e_recv, g_send, g_recv, xe_send, xe_recv,
    c_send, c_recv, ab_send, ab_recv, core_send, core_recv, x_send, x_recv,
    f_send, f_recv, h_send, h_recv,
):
    n_dev = n_row * n_col
    n_z = n_col // 2
    groups = width // LANES
    part = n_col // CHUNKS
    deep = part * width
    r, c = lax.axis_index("row"), lax.axis_index("col")
    per = n_col // n_row
    z, y = lax.div(c, 2), lax.rem(c, 2)
    core, chip = lax.rem(r, 2), lax.div(r, 2)
    near = chip * 2 + 1 - core
    far = (1 - chip) * 2 + core
    cross = (1 - chip) * 2 + 1 - core

    def remote(src, dst, send, recv, target):
        return pltpu.make_async_remote_copy(
            src_ref=src, dst_ref=dst, send_sem=send, recv_sem=recv,
            device_id=target, device_id_type=MESH,
        )

    depth = sbuf.shape[1]
    strip = 32

    def s_copy(i):
        return pltpu.make_async_copy(
            s_hbm.at[pl.ds(i * depth, depth), :], sbuf.at[i % S_SLOTS], s_sem.at[i])

    def convert(i):
        s_copy(i).wait()

        @pl.loop(0, depth // strip)
        def _(n):
            rows = pl.ds(pl.multiple_of(n * strip, strip), strip)
            into = pl.ds(pl.multiple_of(i * depth + n * strip, strip), strip)
            sb[into, :] = sbuf[i % S_SLOTS, rows, :].astype(jnp.bfloat16)

        if i + S_SLOTS < S_COPIES:
            s_copy(i + S_SLOTS).start()

    local = [
        pltpu.make_async_copy(x_hbm, xin, in_sem.at[0]),
        pltpu.make_async_copy(g_hbm, gin, in_sem.at[1]),
        pltpu.make_async_copy(small_hbm, small, in_sem.at[2]),
    ] + [
        pltpu.make_async_copy(
            perm_hbm.at[g], perm.at[:, pl.ds(g * LANES, LANES)], in_sem.at[3 + g])
        for g in range(perm_hbm.shape[0])
    ]
    for copy in local:
        copy.start()
    for i in range(S_SLOTS):
        s_copy(i).start()

    def others(count, mine, body):
        @pl.loop(1, count)
        def _(i):
            body(lax.rem(mine + i, count))

    barrier = pltpu.get_barrier_semaphore()
    others(n_row, r, lambda p: pl.semaphore_signal(
        barrier, inc=1, device_id={"row": p, "col": c}, device_id_type=MESH))
    others(n_col, c, lambda p: pl.semaphore_signal(
        barrier, inc=1, device_id={"row": r, "col": p}, device_id_type=MESH))
    for copy in local:
        copy.wait()
    pl.semaphore_wait(barrier, n_row + n_col - 2)

    def x_row(p, q):
        return remote(
            xin.at[pl.ds(p * n_col, n_col)], xt.at[c, lax.div(q, 2), :, lax.rem(q, 2)],
            row_send.at[0, p], row_recv.at[0, q], {"row": p, "col": c},
        )

    def g_row(p, q):
        return remote(
            gin.at[pl.ds(p * per, per)], grow.at[q],
            row_send.at[1, p], row_recv.at[1, q], {"row": p, "col": c},
        )

    def g_blocks(p, q):
        return remote(
            gin.at[:, p], gblk.at[q],
            row_send.at[2, p], row_recv.at[2, q], {"row": p, "col": c},
        )

    for p in (near, far, cross):
        x_row(p, r).start()
    others(n_row, r, lambda p: g_blocks(p, r).start())
    others(n_row, r, lambda p: g_row(p, r).start())
    xt[c, chip, :, core] = xin[pl.ds(r * n_col, n_col)]
    gblk[r] = gin[:, r]
    grow[r] = gin[pl.ds(r * per, per)]
    n_out = n_dev * TILE
    wide = n_dev * own
    tall = n_row * own

    def unit(u, o):
        if u == 0:
            return xt.at[o, chip]
        return xt.at[o, 1 - chip, pl.ds((u - 1) * part, part)]

    def g_copy(u, o, send, target):
        return remote(
            unit(u, o), unit(u, o), send, g_recv.at[u, o], {"row": r, "col": target})

    def along_z(k, side, d):
        return g_copy(k, c, g_send.at[k, side, d, 0], c + 2 * d if side == 0 else c - 2 * d)

    def along_y(k, side, d, o):
        return g_copy(k, o, g_send.at[k, side, d, 1], z * 2 + 1 - y)

    def spread(k, do):
        do(along_y(k, 0, 0, c))
        for d in range(1, n_z):
            pl.when(z + d < n_z)(lambda d=d: do(along_z(k, 0, d)))
            pl.when(z >= d)(lambda d=d: do(along_z(k, 1, d)))

    def start(copy):
        copy.start()

    def wait_send(copy):
        copy.wait_send()

    def forward(k, do, receive):
        def step(side, d, o):
            copy = along_y(k, side, d, o)
            if receive:
                copy.wait_recv()
            do(copy)

        for d in range(1, n_z):
            pl.when(z + d < n_z)(lambda d=d: step(0, d, c + 2 * d))
            pl.when(z >= d)(lambda d=d: step(1, d, c - 2 * d))

    def blocks_product(k, j):
        rows = pl.ds(k * deep, deep)
        cols = pl.ds(pl.multiple_of(j * width, width), width)
        return dot(xq[k], sb[rows, cols])

    def inner(k):
        return lax.dot_general(
            gsh[k], xq[k], (((1,), (1,)), ((), ())), preferred_element_type=jnp.float32)

    def complete(u):
        for z0 in range(n_z):
            o = z0 * 2 + 1 - y
            along_y(u, 0, 0, o).wait_recv()

    def arrange(k):
        complete(k + 1)
        blocks = [xt[:, :, k * part + b].reshape(n_out, LANES) for b in range(part)]
        turned = dot(perm[...], jnp.concatenate(blocks, axis=1)).astype(jnp.bfloat16)
        for b in range(part):
            for g in range(groups):
                lanes = pl.ds(b * width + g * LANES, LANES)
                xq[k, :, lanes] = turned[g * wide:(g + 1) * wide, b * LANES:(b + 1) * LANES]
        gsh[k, :tall, :] = xq[k, pl.ds(pl.multiple_of(c * tall, tall), tall), :]
        for b in range(part):
            high, low = divmod(k * part + b, n_row)
            block = grow[:, high, low].reshape(n_row * TILE, LANES)
            turned = dot(small[...], block).astype(jnp.bfloat16)
            for g in range(groups):
                lanes = pl.ds(b * width + g * LANES, LANES)
                gsh[k, tall:, lanes] = turned[g * tall:(g + 1) * tall]

    def product(k):
        @pl.loop(0, n_row)
        def _(j):
            if k == 0:
                acc[j] = blocks_product(k, j)
            else:
                acc[j] += blocks_product(k, j)

    def e_copy(p, q):
        return remote(gblk.at[:, p], gt.at[q], e_send.at[p], e_recv.at[q], {"row": r, "col": p})

    x_row(near, near).wait_recv()
    spread(0, start)
    convert(0)
    convert(1)
    x_row(far, far).wait_recv()
    x_row(cross, cross).wait_recv()
    for k in range(CHUNKS):
        spread(k + 1, start)
    others(n_row, r, lambda q: g_blocks(q, q).wait_recv())
    others(n_col, c, lambda p: e_copy(p, c).start())
    gt[c] = gblk[:, c]
    forward(0, start, True)
    convert(2)
    convert(3)
    others(n_row, r, lambda q: g_row(q, q).wait_recv())
    gram = None
    for k in range(CHUNKS):
        forward(k + 1, start, True)
        convert(S_COPIES // 2 + k)
        if k == 0:
            complete(0)
        else:
            arrange(k - 1)
            gram = inner(k - 1) if gram is None else gram + inner(k - 1)
            product(k - 1)

    last = CHUNKS - 1
    arrange(last)
    holder = lax.div(c, per)

    def xe_copy(p):
        block = lax.rem(c, per) * n_row + p
        lanes = pl.ds(pl.multiple_of(lax.rem(block, part) * width, width), width)
        return remote(
            xq.at[lax.div(block, part), :, lanes], xe,
            xe_send.at[p], xe_recv, {"row": p, "col": c})

    @pl.when(r == holder)
    def _():
        others(n_row, r, lambda p: xe_copy(p).start())
        block = lax.rem(c, per) * n_row + r
        lanes = pl.ds(pl.multiple_of(lax.rem(block, part) * width, width), width)
        xe[...] = xq[lax.div(block, part), :, lanes]

    cbuf[r] = gram + inner(last)

    def c_copy(p, q):
        return remote(cbuf.at[q], cbuf.at[q], c_send.at[p], c_recv.at[q], {"row": p, "col": c})

    others(n_row, r, lambda p: c_copy(p, r).start())

    def core_copy(i, j):
        return remote(acc.at[j], rbuf.at[i], core_send.at[i], core_recv.at[i],
                      {"row": near, "col": c})

    acc[cross] += blocks_product(last, cross)
    core_copy(0, cross).start()
    acc[near] += blocks_product(last, near)
    core_copy(1, near).start()

    others(n_row, r, lambda q: c_copy(q, q).wait_recv())
    total = cbuf[0]
    for q in range(1, n_row):
        total = total + cbuf[q]
    ab[c] = total

    def ab_copy(p, q):
        return remote(ab.at[q], ab.at[q], ab_send.at[p], ab_recv.at[q], {"row": r, "col": p})

    others(n_col, c, lambda p: ab_copy(p, c).start())

    acc[far] += blocks_product(last, far)
    core_copy(0, cross).wait_recv()
    xout[...] = (acc[far] + rbuf[0]).astype(jnp.bfloat16)
    x_copy = remote(xout, xbuf, x_send, x_recv, {"row": far, "col": c})
    x_copy.start()
    acc[r] += blocks_product(last, r)

    others(n_col, c, lambda q: e_copy(q, q).wait_recv())
    turned = dot(perm[...], gt[...].reshape(n_out, LANES)).astype(jnp.bfloat16)
    for g in range(groups):
        ge[:, g * LANES:(g + 1) * LANES] = turned[g * wide:(g + 1) * wide]
    pl.when(r != holder)(lambda: xe_copy(r).wait_recv())

    others(n_col, c, lambda q: ab_copy(q, q).wait_recv())
    orb_orb = ab[:, :tall, :].reshape(wide, wide)
    orb_grad = ab[:, tall:, :].reshape(wide, wide).T

    def accurate(left, right):
        high = left.astype(jnp.bfloat16)
        low = (left - high.astype(jnp.float32)).astype(jnp.bfloat16)
        return dot(high, right) + dot(low, right)

    rest = ge[...].astype(jnp.float32) - 0.5 * (
        accurate(orb_orb, ge[...]) + accurate(orb_grad, xe[...]))
    core_copy(1, near).wait_recv()
    rest = rest - (acc[r] + rbuf[1])
    x_copy.wait_recv()
    result = (rest - xbuf[...].astype(jnp.float32)).astype(jnp.bfloat16)
    stack = jnp.concatenate([result[:, g * LANES:(g + 1) * LANES] for g in range(groups)], axis=0)
    tiles = lax.dot_general(
        perm[...], stack, (((0,), (0,)), ((), ())), preferred_element_type=jnp.float32)
    fbuf[...] = tiles.astype(jnp.bfloat16).reshape(n_col, n_row, TILE, LANES)

    def f_copy(p, q):
        return remote(fbuf.at[p], fmid.at[q], f_send.at[p], f_recv.at[q], {"row": r, "col": p})

    def h_copy(p, q):
        return remote(
            fmid.at[:, p], out.at[:, q], h_send.at[p], h_recv.at[q], {"row": p, "col": c})

    others(n_col, c, lambda p: f_copy(p, c).start())
    fmid[c] = fbuf[c]
    others(n_col, c, lambda q: f_copy(q, q).wait_recv())
    others(n_row, r, lambda p: h_copy(p, r).start())
    out[:, r] = fmid[:, r]

    for sent in (x_row, g_row, g_blocks):
        others(n_row, r, lambda p, sent=sent: sent(p, r).wait_send())

    @pl.when(r == holder)
    def _():
        others(n_row, r, lambda p: xe_copy(p).wait_send())

    others(n_row, r, lambda p: c_copy(p, r).wait_send())
    others(n_col, c, lambda p: ab_copy(p, c).wait_send())
    others(n_col, c, lambda p: e_copy(p, c).wait_send())
    for k in range(CHUNKS + 1):
        spread(k, wait_send)
        forward(k, wait_send, False)
    core_copy(0, cross).wait_send()
    core_copy(1, near).wait_send()
    x_copy.wait_send()
    others(n_col, c, lambda p: f_copy(p, c).wait_send())
    others(n_row, r, lambda q: h_copy(q, q).wait_recv())
    others(n_row, r, lambda p: h_copy(p, r).wait_send())


def kernel_body(n_row, n_col, orbitals, gradient, stored):
    own, n_orb = orbitals.shape
    n_dev = n_row * n_col
    width = n_orb // n_dev
    groups = width // LANES
    n_pw = own * n_dev
    tall = n_row * own
    deep = n_orb // n_row // CHUNKS

    def tiled(rows):
        shaped = rows.reshape(own, n_dev, groups, LANES)
        return shaped.transpose(1, 2, 0, 3).reshape(n_dev, TILE, LANES)

    def gather_rows(blocks, rows):
        perm = np.zeros((blocks * TILE, blocks * TILE), np.float32)
        for at in range(blocks * TILE):
            group, rest = divmod(at, blocks * rows)
            block, row = divmod(rest, rows)
            perm[at, block * TILE + group * rows + row] = 1.0
        if perm.shape[1] > LANES:
            perm = perm.reshape(perm.shape[0], -1, LANES).transpose(1, 0, 2)
        return jnp.asarray(perm, jnp.bfloat16)

    bf16, f32 = jnp.bfloat16, jnp.float32
    dma = pltpu.SemaphoreType.DMA
    tiles = pl.pallas_call(
        functools.partial(kernel, n_row, n_col, own, width),
        out_shape=jax.ShapeDtypeStruct((n_col, n_row, TILE, LANES), bf16),
        in_specs=[pl.BlockSpec(memory_space=pl.ANY)] * 5,
        out_specs=pl.BlockSpec(memory_space=pltpu.VMEM),
        scratch_shapes=[
            pltpu.VMEM((n_dev, TILE, LANES), bf16),
            pltpu.VMEM((n_col, n_row, TILE, LANES), bf16),
            pltpu.VMEM((n_row * TILE, n_row * TILE), bf16),
            pltpu.VMEM((S_SLOTS, stored.shape[0] // S_COPIES, stored.shape[1]), f32),
            pltpu.VMEM(stored.shape, bf16),
            pltpu.VMEM((n_col, 2, n_col, 2, TILE, LANES), bf16),
            pltpu.VMEM((n_row, n_col // n_row, n_row, TILE, LANES), bf16),
            pltpu.VMEM((n_row, n_col, TILE, LANES), bf16),
            pltpu.VMEM((n_col, n_row, TILE, LANES), bf16),
            pltpu.VMEM((CHUNKS, n_pw, deep), bf16),
            pltpu.VMEM((CHUNKS, 2 * tall, deep), bf16),
            pltpu.VMEM((n_row, n_pw, width), f32),
            pltpu.VMEM((2, n_pw, width), f32),
            pltpu.VMEM((n_pw, width), bf16),
            pltpu.VMEM((n_pw, width), bf16),
            pltpu.VMEM((n_pw, width), bf16),
            pltpu.VMEM((n_pw, width), bf16),
            pltpu.VMEM((n_dev * TILE, n_dev * TILE), bf16),
            pltpu.VMEM((n_row, 2 * tall, n_pw), f32),
            pltpu.VMEM((n_col, 2 * tall, n_pw), f32),
            pltpu.VMEM((n_col, n_row, TILE, LANES), bf16),
            pltpu.VMEM((n_col, n_row, TILE, LANES), bf16),
            dma((3 + n_dev * TILE // LANES,)), dma((S_COPIES,)), dma((3, n_row)), dma((3, n_row)),
            dma((n_col,)), dma((n_col,)),
            dma((CHUNKS + 1, 2, n_col // 2, 2)), dma((CHUNKS + 1, n_col)), dma((n_row,)), dma(()),
            dma((n_row,)), dma((n_row,)), dma((n_col,)), dma((n_col,)),
            dma((2,)), dma((2,)), dma(()), dma(()),
            dma((n_col,)), dma((n_col,)), dma((n_row,)), dma((n_row,)),
        ],
        compiler_params=pltpu.CompilerParams(
            collective_id=0, has_side_effects=True, vmem_limit_bytes=56 * 1024 * 1024),
        cost_estimate=pl.CostEstimate(
            flops=2 * n_pw * stored.size, bytes_accessed=4 * stored.size, transcendentals=0),
    )(tiled(orbitals), tiled(gradient).reshape(n_col, n_row, TILE, LANES), gather_rows(n_dev, own), gather_rows(n_row, own), stored)
    shaped = tiles.reshape(n_dev, groups, own, LANES)
    return shaped.transpose(2, 0, 1, 3).reshape(own, n_orb)


def body(orbitals, gradient, stored):
    n_row = lax.axis_size("row")
    n_col = lax.axis_size("col")
    own, n_orb = orbitals.shape
    n_dev = n_row * n_col
    width = n_orb // n_dev
    fits = (
        n_row == 4 and n_col % CHUNKS == 0 and n_col % n_row == 0 and width % LANES == 0
        and own * width == TILE * LANES and own * n_row == TILE
        and own * n_dev == LANES and stored.shape[0] % S_COPIES == 0
        and stored.size * 4 <= 32 * 1024 * 1024
    )
    if fits:
        return kernel_body(n_row, n_col, orbitals, gradient, stored)
    return general_body(orbitals, gradient, stored)


def solution(mesh):
    return jax.shard_map(
        body,
        mesh=mesh,
        in_specs=(P(("row", "col"), None), P(("row", "col"), None), P("row", "col")),
        out_specs=P(("row", "col"), None),
        check_vma=False,
    )
```

```python
import functools

import jax
import jax.numpy as jnp
import numpy as np
from jax import lax
from jax.experimental import pallas as pl
from jax.experimental.pallas import tpu as pltpu
from jax.sharding import PartitionSpec as P

MESH = pl.DeviceIdType.MESH
LANES = 128
TILE = 16
CHUNKS = 4
S_COPIES = 8
S_SLOTS = 6


def reorder(panel, outer, inner):
    width = panel.shape[1]
    shaped = panel.reshape(outer, inner, -1, width)
    return jnp.swapaxes(shaped, 0, 1).reshape(-1, width)


def inner_product(left, right):
    return lax.dot_general(
        left, right, (((0,), (0,)), ((), ())), preferred_element_type=jnp.float32
    )


def dot(left, right):
    return jnp.dot(left, right, preferred_element_type=jnp.float32)


def general_body(orbitals, gradient, stored):
    n_row = lax.axis_size("row")
    n_col = lax.axis_size("col")
    orb_q, grad_q = (
        lax.all_to_all(orbitals, "row", split_axis=1, concat_axis=0, tiled=True),
        lax.all_to_all(gradient, "row", split_axis=1, concat_axis=0, tiled=True),
    )
    orb_q, grad_q = (
        lax.all_gather(orb_q, "col", axis=0, tiled=True),
        lax.all_gather(grad_q, "col", axis=0, tiled=True),
    )
    orb_q = reorder(orb_q, n_col, n_row)
    grad_q = reorder(grad_q, n_col, n_row)
    orb_o, grad_o = (
        lax.all_to_all(orbitals, "col", split_axis=1, concat_axis=0, tiled=True),
        lax.all_to_all(gradient, "col", split_axis=1, concat_axis=0, tiled=True),
    )
    orb_o, grad_o = (
        lax.all_gather(orb_o, "row", axis=0, tiled=True),
        lax.all_gather(grad_o, "row", axis=0, tiled=True),
    )
    half = (0.5 * inner_product(orb_q, grad_o) + 0.5 * stored).astype(jnp.bfloat16)
    half_mirror = (0.5 * inner_product(grad_q, orb_o) + 0.5 * stored).astype(jnp.bfloat16)
    share = lax.psum_scatter(
        dot(orb_q, half) + dot(orb_q, half_mirror), "row", scatter_dimension=0, tiled=True
    )
    correction = lax.all_to_all(share, "col", split_axis=0, concat_axis=1, tiled=True)
    return (gradient.astype(jnp.float32) - correction).astype(jnp.bfloat16)


def kernel(
    n_row, n_col, own, width,
    x_hbm, g_hbm, perm_hbm, small_hbm, s_hbm, out,
    xg, small, sbuf, sb, rowbuf, xq, gsh, acc, rbuf, xout, xbuf, ebuf, xe, ge, perm, cbuf, ab, fbuf,
    in_sem, s_sem, row_send, row_recv, e_send, e_recv, g_send, g_recv,
    c_send, c_recv, ab_send, ab_recv, core_send, core_recv, x_send, x_recv, f_send, f_recv,
):
    n_dev = n_row * n_col
    n_z = n_col // 2
    groups = width // LANES
    part = n_col // CHUNKS
    deep = part * width
    r, c = lax.axis_index("row"), lax.axis_index("col")
    me = c * n_row + r
    z, y = lax.div(c, 2), lax.rem(c, 2)
    core, chip = lax.rem(r, 2), lax.div(r, 2)
    near = chip * 2 + 1 - core
    far = (1 - chip) * 2 + core
    cross = (1 - chip) * 2 + 1 - core

    def device(d):
        return {"row": lax.rem(d, n_row), "col": lax.div(d, n_row)}

    def remote(src, dst, send, recv, target):
        return pltpu.make_async_remote_copy(
            src_ref=src, dst_ref=dst, send_sem=send, recv_sem=recv,
            device_id=target, device_id_type=MESH,
        )

    depth = sbuf.shape[1]
    strip = 32

    def s_copy(i):
        return pltpu.make_async_copy(
            s_hbm.at[pl.ds(i * depth, depth), :], sbuf.at[i % S_SLOTS], s_sem.at[i])

    def convert(i):
        s_copy(i).wait()

        @pl.loop(0, depth // strip)
        def _(n):
            rows = pl.ds(pl.multiple_of(n * strip, strip), strip)
            into = pl.ds(pl.multiple_of(i * depth + n * strip, strip), strip)
            sb[into, :] = sbuf[i % S_SLOTS, rows, :].astype(jnp.bfloat16)

        if i + S_SLOTS < S_COPIES:
            s_copy(i + S_SLOTS).start()

    local = [
        pltpu.make_async_copy(x_hbm, xg.at[:, 0], in_sem.at[0]),
        pltpu.make_async_copy(g_hbm, xg.at[:, 1], in_sem.at[1]),
        pltpu.make_async_copy(small_hbm, small, in_sem.at[2]),
    ] + [
        pltpu.make_async_copy(
            perm_hbm.at[g], perm.at[:, pl.ds(g * LANES, LANES)], in_sem.at[3 + g])
        for g in range(perm_hbm.shape[0])
    ]
    for copy in local:
        copy.start()
    for i in range(S_SLOTS):
        s_copy(i).start()

    def others(count, mine, body):
        @pl.loop(1, count)
        def _(i):
            body(lax.rem(mine + i, count))

    barrier = pltpu.get_barrier_semaphore()
    others(n_dev, me, lambda d: pl.semaphore_signal(
        barrier, inc=1, device_id=device(d), device_id_type=MESH))
    for copy in local:
        copy.wait()
    pl.semaphore_wait(barrier, n_dev - 1)

    def row_copy(p, q):
        return remote(
            xg.at[pl.ds(p * n_col, n_col)], rowbuf.at[q],
            row_send.at[p], row_recv.at[q], {"row": p, "col": c},
        )

    others(n_row, r, lambda p: row_copy(p, r).start())
    rowbuf[r] = xg[pl.ds(r * n_col, n_col)]

    def e_copy(d, s):
        return remote(xg.at[d], ebuf.at[s], e_send.at[d], e_recv.at[s], device(d))

    others(n_dev, me, lambda d: e_copy(d, me).start())
    ebuf[me] = xg[me]
    n_out = n_dev * TILE
    wide = n_dev * own
    tall = n_row * own
    for i in range(S_COPIES // 2):
        convert(i)

    others(n_row, r, lambda q: row_copy(q, q).wait_recv())

    def shard(k, o):
        return xq.at[k, pl.ds(pl.multiple_of(o * tall, tall), tall), :]

    def g_copy(k, o, send, target):
        return remote(
            shard(k, o), shard(k, o), send, g_recv.at[k, o], {"row": r, "col": target})

    up, down = n_z // 2, n_z - 1 - n_z // 2

    def along_z(k, side, d):
        return g_copy(k, c, g_send.at[k, side, d, 0], c + 2 * d if side == 0 else c - 2 * d)

    def along_y(k, side, d, o):
        return g_copy(k, o, g_send.at[k, side, d, 1], z * 2 + 1 - y)

    def relay(k, side, d, o, t):
        return g_copy(k, o, g_send.at[k, side, d, 2 + t], 2 * t + y)

    def spread(k, do):
        do(along_y(k, 0, 0, c))
        for d in range(1, n_z):
            to = z + d
            pl.when((to < n_z) & ((z >= up) | (to <= up)))(lambda d=d: do(along_z(k, 0, d)))
            to = z - d
            pl.when((to >= 0) & ((z <= down) | (to >= down)))(lambda d=d: do(along_z(k, 1, d)))

    def start(copy):
        copy.start()

    def wait_send(copy):
        copy.wait_send()

    def post(k):
        mine = pl.ds(pl.multiple_of(c * tall, tall), tall)
        for b in range(part):
            for t in range(2):
                block = rowbuf[:, k * part + b, t].reshape(n_row * TILE, LANES)
                turned = dot(small[...], block).astype(jnp.bfloat16)
                for g in range(groups):
                    piece = turned[g * tall:(g + 1) * tall]
                    lanes = pl.ds(b * width + g * LANES, LANES)
                    gsh[k, t * tall:(t + 1) * tall, lanes] = piece
                    if t == 0:
                        xq[k, mine, lanes] = piece
        spread(k, start)

    def forward(k, do, receive):
        def step(side, d, o):
            copy = along_y(k, side, d, o)
            if receive:
                copy.wait_recv()
            if side == 0:
                turn, targets = down, range(down)
            else:
                turn, targets = up, range(up + 1, n_z)

            @pl.when(z == turn)
            def _():
                for t in targets:
                    do(relay(k, side, d, o, t))

            do(copy)

        for d in range(1, n_z):
            pl.when(z + d < n_z)(lambda d=d: step(0, d, c + 2 * d))
            pl.when(z >= d)(lambda d=d: step(1, d, c - 2 * d))

    def blocks_product(k, j):
        rows = pl.ds(k * deep, deep)
        cols = pl.ds(pl.multiple_of(j * width, width), width)
        return dot(xq[k], sb[rows, cols])

    def inner(k):
        return lax.dot_general(
            gsh[k], xq[k], (((1,), (1,)), ((), ())), preferred_element_type=jnp.float32)

    def complete(k):
        for z0 in range(n_z):
            o = z0 * 2 + 1 - y
            along_y(k, 0, 0, o).wait_recv()

    def product(k):
        @pl.loop(0, n_row)
        def _(j):
            if k == 0:
                acc[j] = blocks_product(k, j)
            else:
                acc[j] += blocks_product(k, j)

    for k in range(CHUNKS):
        post(k)
    gram = None
    for k in range(CHUNKS + 1):
        if k < CHUNKS:
            forward(k, start, True)
        piece = S_COPIES // 2 + k
        if piece < S_COPIES:
            convert(piece)
        if 1 <= k < CHUNKS:
            complete(k - 1)
            gram = inner(k - 1) if gram is None else gram + inner(k - 1)
            product(k - 1)

    last = CHUNKS - 1
    complete(last)
    cbuf[r] = gram + inner(last)

    def c_copy(p, q):
        return remote(cbuf.at[q], cbuf.at[q], c_send.at[p], c_recv.at[q], {"row": p, "col": c})

    others(n_row, r, lambda p: c_copy(p, r).start())

    def core_copy(i, j):
        return remote(acc.at[j], rbuf.at[i], core_send.at[i], core_recv.at[i],
                      {"row": near, "col": c})

    acc[cross] += blocks_product(last, cross)
    core_copy(0, cross).start()
    acc[near] += blocks_product(last, near)
    core_copy(1, near).start()

    others(n_row, r, lambda q: c_copy(q, q).wait_recv())
    total = cbuf[0]
    for q in range(1, n_row):
        total = total + cbuf[q]
    ab[c] = total

    def ab_copy(p, q):
        return remote(ab.at[q], ab.at[q], ab_send.at[p], ab_recv.at[q], {"row": r, "col": p})

    others(n_col, c, lambda p: ab_copy(p, c).start())

    acc[far] += blocks_product(last, far)
    core_copy(0, cross).wait_recv()
    xout[...] = (acc[far] + rbuf[0]).astype(jnp.bfloat16)
    x_copy = remote(xout, xbuf, x_send, x_recv, {"row": far, "col": c})
    x_copy.start()
    acc[r] += blocks_product(last, r)

    others(n_dev, me, lambda s: e_copy(s, s).wait_recv())
    for t, dest in ((0, xe), (1, ge)):
        turned = dot(perm[...], ebuf[:, t].reshape(n_out, LANES)).astype(jnp.bfloat16)
        for g in range(groups):
            dest[:, g * LANES:(g + 1) * LANES] = turned[g * wide:(g + 1) * wide]

    others(n_col, c, lambda q: ab_copy(q, q).wait_recv())
    orb_orb = ab[:, :tall, :].reshape(wide, wide)
    orb_grad = ab[:, tall:, :].reshape(wide, wide).T

    def accurate(left, right):
        high = left.astype(jnp.bfloat16)
        low = (left - high.astype(jnp.float32)).astype(jnp.bfloat16)
        return dot(high, right) + dot(low, right)

    rest = ge[...].astype(jnp.float32) - 0.5 * (
        accurate(orb_orb, ge[...]) + accurate(orb_grad, xe[...]))
    core_copy(1, near).wait_recv()
    rest = rest - (acc[r] + rbuf[1])
    x_copy.wait_recv()
    result = (rest - xbuf[...].astype(jnp.float32)).astype(jnp.bfloat16)
    stack = jnp.concatenate([result[:, g * LANES:(g + 1) * LANES] for g in range(groups)], axis=0)
    tiles = lax.dot_general(
        perm[...], stack, (((0,), (0,)), ((), ())), preferred_element_type=jnp.float32)
    fbuf[...] = tiles.astype(jnp.bfloat16).reshape(n_dev, TILE, LANES)

    def f_copy(d, s):
        return remote(fbuf.at[d], out.at[s], f_send.at[d], f_recv.at[s], device(d))

    others(n_dev, me, lambda d: f_copy(d, me).start())
    out[me] = fbuf[me]

    others(n_row, r, lambda p: row_copy(p, r).wait_send())
    others(n_row, r, lambda p: c_copy(p, r).wait_send())
    others(n_col, c, lambda p: ab_copy(p, c).wait_send())
    others(n_dev, me, lambda d: e_copy(d, me).wait_send())
    for k in range(CHUNKS):
        spread(k, wait_send)
        forward(k, wait_send, False)
    core_copy(0, cross).wait_send()
    core_copy(1, near).wait_send()
    x_copy.wait_send()
    others(n_dev, me, lambda s: f_copy(s, s).wait_recv())
    others(n_dev, me, lambda d: f_copy(d, me).wait_send())


def kernel_body(n_row, n_col, orbitals, gradient, stored):
    own, n_orb = orbitals.shape
    n_dev = n_row * n_col
    width = n_orb // n_dev
    groups = width // LANES
    n_pw = own * n_dev
    tall = n_row * own
    deep = n_orb // n_row // CHUNKS

    def tiled(rows):
        shaped = rows.reshape(own, n_dev, groups, LANES)
        return shaped.transpose(1, 2, 0, 3).reshape(n_dev, TILE, LANES)

    def gather_rows(blocks, rows):
        perm = np.zeros((blocks * TILE, blocks * TILE), np.float32)
        for at in range(blocks * TILE):
            group, rest = divmod(at, blocks * rows)
            block, row = divmod(rest, rows)
            perm[at, block * TILE + group * rows + row] = 1.0
        if perm.shape[1] > LANES:
            perm = perm.reshape(perm.shape[0], -1, LANES).transpose(1, 0, 2)
        return jnp.asarray(perm, jnp.bfloat16)

    bf16, f32 = jnp.bfloat16, jnp.float32
    dma = pltpu.SemaphoreType.DMA
    tiles = pl.pallas_call(
        functools.partial(kernel, n_row, n_col, own, width),
        out_shape=jax.ShapeDtypeStruct((n_dev, TILE, LANES), bf16),
        in_specs=[pl.BlockSpec(memory_space=pl.ANY)] * 5,
        out_specs=pl.BlockSpec(memory_space=pltpu.VMEM),
        scratch_shapes=[
            pltpu.VMEM((n_dev, 2, TILE, LANES), bf16),
            pltpu.VMEM((n_row * TILE, n_row * TILE), bf16),
            pltpu.VMEM((S_SLOTS, stored.shape[0] // S_COPIES, stored.shape[1]), f32),
            pltpu.VMEM(stored.shape, bf16),
            pltpu.VMEM((n_row, n_col, 2, TILE, LANES), bf16),
            pltpu.VMEM((CHUNKS, n_pw, deep), bf16),
            pltpu.VMEM((CHUNKS, 2 * tall, deep), bf16),
            pltpu.VMEM((n_row, n_pw, width), f32),
            pltpu.VMEM((2, n_pw, width), f32),
            pltpu.VMEM((n_pw, width), bf16),
            pltpu.VMEM((n_pw, width), bf16),
            pltpu.VMEM((n_dev, 2, TILE, LANES), bf16),
            pltpu.VMEM((n_pw, width), bf16),
            pltpu.VMEM((n_pw, width), bf16),
            pltpu.VMEM((n_dev * TILE, n_dev * TILE), bf16),
            pltpu.VMEM((n_row, 2 * tall, n_pw), f32),
            pltpu.VMEM((n_col, 2 * tall, n_pw), f32),
            pltpu.VMEM((n_dev, TILE, LANES), bf16),
            dma((3 + n_dev * TILE // LANES,)), dma((S_COPIES,)), dma((n_row,)), dma((n_row,)), dma((n_dev,)), dma((n_dev,)),
            dma((CHUNKS, 2, n_col // 2, 2 + n_col // 2)), dma((CHUNKS, n_col)),
            dma((n_row,)), dma((n_row,)), dma((n_col,)), dma((n_col,)),
            dma((2,)), dma((2,)), dma(()), dma(()), dma((n_dev,)), dma((n_dev,)),
        ],
        compiler_params=pltpu.CompilerParams(
            collective_id=0, has_side_effects=True, vmem_limit_bytes=56 * 1024 * 1024),
        cost_estimate=pl.CostEstimate(
            flops=2 * n_pw * stored.size, bytes_accessed=4 * stored.size, transcendentals=0),
    )(tiled(orbitals), tiled(gradient), gather_rows(n_dev, own), gather_rows(n_row, own), stored)
    shaped = tiles.reshape(n_dev, groups, own, LANES)
    return shaped.transpose(2, 0, 1, 3).reshape(own, n_orb)


def body(orbitals, gradient, stored):
    n_row = lax.axis_size("row")
    n_col = lax.axis_size("col")
    own, n_orb = orbitals.shape
    n_dev = n_row * n_col
    width = n_orb // n_dev
    fits = (
        n_row == 4 and n_col % CHUNKS == 0 and width % LANES == 0
        and own * width == TILE * LANES and own * n_row == TILE
        and own * n_dev == LANES and stored.shape[0] % S_COPIES == 0
        and stored.size * 4 <= 32 * 1024 * 1024
    )
    if fits:
        return kernel_body(n_row, n_col, orbitals, gradient, stored)
    return general_body(orbitals, gradient, stored)


def solution(mesh):
    return jax.shard_map(
        body,
        mesh=mesh,
        in_specs=(P(("row", "col"), None), P(("row", "col"), None), P("row", "col")),
        out_specs=P(("row", "col"), None),
        check_vma=False,
    )
```

```python
import functools

import jax
import jax.numpy as jnp
import numpy as np
from jax import lax
from jax.experimental import pallas as pl
from jax.experimental.pallas import tpu as pltpu
from jax.sharding import PartitionSpec as P

MESH = pl.DeviceIdType.MESH
LANES = 128
TILE = 16
CHUNKS = 4
S_COPIES = 8
S_SLOTS = 6


def reorder(panel, outer, inner):
    width = panel.shape[1]
    shaped = panel.reshape(outer, inner, -1, width)
    return jnp.swapaxes(shaped, 0, 1).reshape(-1, width)


def inner_product(left, right):
    return lax.dot_general(
        left, right, (((0,), (0,)), ((), ())), preferred_element_type=jnp.float32
    )


def dot(left, right):
    return jnp.dot(left, right, preferred_element_type=jnp.float32)


def general_body(orbitals, gradient, stored):
    n_row = lax.axis_size("row")
    n_col = lax.axis_size("col")
    orb_q, grad_q = (
        lax.all_to_all(orbitals, "row", split_axis=1, concat_axis=0, tiled=True),
        lax.all_to_all(gradient, "row", split_axis=1, concat_axis=0, tiled=True),
    )
    orb_q, grad_q = (
        lax.all_gather(orb_q, "col", axis=0, tiled=True),
        lax.all_gather(grad_q, "col", axis=0, tiled=True),
    )
    orb_q = reorder(orb_q, n_col, n_row)
    grad_q = reorder(grad_q, n_col, n_row)
    orb_o, grad_o = (
        lax.all_to_all(orbitals, "col", split_axis=1, concat_axis=0, tiled=True),
        lax.all_to_all(gradient, "col", split_axis=1, concat_axis=0, tiled=True),
    )
    orb_o, grad_o = (
        lax.all_gather(orb_o, "row", axis=0, tiled=True),
        lax.all_gather(grad_o, "row", axis=0, tiled=True),
    )
    half = (0.5 * inner_product(orb_q, grad_o) + 0.5 * stored).astype(jnp.bfloat16)
    half_mirror = (0.5 * inner_product(grad_q, orb_o) + 0.5 * stored).astype(jnp.bfloat16)
    share = lax.psum_scatter(
        dot(orb_q, half) + dot(orb_q, half_mirror), "row", scatter_dimension=0, tiled=True
    )
    correction = lax.all_to_all(share, "col", split_axis=0, concat_axis=1, tiled=True)
    return (gradient.astype(jnp.float32) - correction).astype(jnp.bfloat16)


def kernel(
    n_row, n_col, own, width,
    x_hbm, g_hbm, perm_hbm, back_hbm, small_hbm, s_hbm, out,
    xg, small, sbuf, sb, rowbuf, xq, gsh, acc, rbuf, xout, xbuf, ebuf, xe, ge, perm, back, cbuf, ab, fbuf,
    in_sem, s_sem, row_send, row_recv, e_send, e_recv, g_send, g_recv,
    c_send, c_recv, ab_send, ab_recv, core_send, core_recv, x_send, x_recv, f_send, f_recv,
):
    n_dev = n_row * n_col
    n_z = n_col // 2
    groups = width // LANES
    part = n_col // CHUNKS
    deep = part * width
    r, c = lax.axis_index("row"), lax.axis_index("col")
    me = c * n_row + r
    z, y = lax.div(c, 2), lax.rem(c, 2)
    core, chip = lax.rem(r, 2), lax.div(r, 2)
    near = chip * 2 + 1 - core
    far = (1 - chip) * 2 + core
    cross = (1 - chip) * 2 + 1 - core

    def device(d):
        return {"row": lax.rem(d, n_row), "col": lax.div(d, n_row)}

    def remote(src, dst, send, recv, target):
        return pltpu.make_async_remote_copy(
            src_ref=src, dst_ref=dst, send_sem=send, recv_sem=recv,
            device_id=target, device_id_type=MESH,
        )

    depth = sbuf.shape[1]
    strip = 32

    def s_copy(i):
        return pltpu.make_async_copy(
            s_hbm.at[pl.ds(i * depth, depth), :], sbuf.at[i % S_SLOTS], s_sem.at[i])

    def convert(i):
        s_copy(i).wait()

        @pl.loop(0, depth // strip)
        def _(n):
            rows = pl.ds(pl.multiple_of(n * strip, strip), strip)
            into = pl.ds(pl.multiple_of(i * depth + n * strip, strip), strip)
            sb[into, :] = sbuf[i % S_SLOTS, rows, :].astype(jnp.bfloat16)

        if i + S_SLOTS < S_COPIES:
            s_copy(i + S_SLOTS).start()

    local = [
        pltpu.make_async_copy(x_hbm, xg.at[:, 0], in_sem.at[0]),
        pltpu.make_async_copy(g_hbm, xg.at[:, 1], in_sem.at[1]),
        pltpu.make_async_copy(small_hbm, small, in_sem.at[2]),
    ] + [
        pltpu.make_async_copy(
            perm_hbm.at[g], perm.at[:, pl.ds(g * LANES, LANES)], in_sem.at[3 + g])
        for g in range(perm_hbm.shape[0])
    ] + [
        pltpu.make_async_copy(
            back_hbm.at[g], back.at[:, pl.ds(g * LANES, LANES)],
            in_sem.at[3 + perm_hbm.shape[0] + g])
        for g in range(perm_hbm.shape[0])
    ]
    for copy in local:
        copy.start()
    for i in range(S_SLOTS):
        s_copy(i).start()

    def others(count, mine, body):
        @pl.loop(1, count)
        def _(i):
            body(lax.rem(mine + i, count))

    barrier = pltpu.get_barrier_semaphore()
    others(n_dev, me, lambda d: pl.semaphore_signal(
        barrier, inc=1, device_id=device(d), device_id_type=MESH))
    for copy in local:
        copy.wait()
    pl.semaphore_wait(barrier, n_dev - 1)

    def row_copy(p, q):
        return remote(
            xg.at[pl.ds(p * n_col, n_col)], rowbuf.at[q],
            row_send.at[p], row_recv.at[q], {"row": p, "col": c},
        )

    others(n_row, r, lambda p: row_copy(p, r).start())
    rowbuf[r] = xg[pl.ds(r * n_col, n_col)]

    def e_copy(d, s):
        return remote(xg.at[d], ebuf.at[s], e_send.at[d], e_recv.at[s], device(d))

    others(n_dev, me, lambda d: e_copy(d, me).start())
    ebuf[me] = xg[me]
    n_out = n_dev * TILE
    wide = n_dev * own
    tall = n_row * own
    others(n_row, r, lambda q: row_copy(q, q).wait_recv())

    def shard(k, o):
        return xq.at[k, pl.ds(pl.multiple_of(o * tall, tall), tall), :]

    def g_copy(k, o, send, target):
        return remote(
            shard(k, o), shard(k, o), send, g_recv.at[k, o], {"row": r, "col": target})

    def along_z(k, side, d):
        return g_copy(k, c, g_send.at[k, side, d, 0], c + 2 * d if side == 0 else c - 2 * d)

    def along_y(k, side, d, o):
        return g_copy(k, o, g_send.at[k, side, d, 1], z * 2 + 1 - y)

    def spread(k, do):
        do(along_y(k, 0, 0, c))
        for d in range(1, n_z):
            pl.when(z + d < n_z)(lambda d=d: do(along_z(k, 0, d)))
            pl.when(z >= d)(lambda d=d: do(along_z(k, 1, d)))

    def start(copy):
        copy.start()

    def wait_send(copy):
        copy.wait_send()

    def post(k):
        mine = pl.ds(pl.multiple_of(c * tall, tall), tall)
        for b in range(part):
            for t in range(2):
                block = rowbuf[:, k * part + b, t].reshape(n_row * TILE, LANES)
                turned = dot(small[...], block).astype(jnp.bfloat16)
                for g in range(groups):
                    piece = turned[g * tall:(g + 1) * tall]
                    lanes = pl.ds(b * width + g * LANES, LANES)
                    gsh[k, t * tall:(t + 1) * tall, lanes] = piece
                    if t == 0:
                        xq[k, mine, lanes] = piece
        spread(k, start)

    def forward(k, do, receive):
        def step(side, d, o):
            copy = along_y(k, side, d, o)
            if receive:
                copy.wait_recv()
            do(copy)

        for d in range(1, n_z):
            pl.when(z + d < n_z)(lambda d=d: step(0, d, c + 2 * d))
            pl.when(z >= d)(lambda d=d: step(1, d, c - 2 * d))

    def blocks_product(k, j):
        rows = pl.ds(k * deep, deep)
        cols = pl.ds(pl.multiple_of(j * width, width), width)
        return dot(xq[k], sb[rows, cols])

    def inner(k):
        return lax.dot_general(
            gsh[k], xq[k], (((1,), (1,)), ((), ())), preferred_element_type=jnp.float32)

    def complete(k):
        for z0 in range(n_z):
            o = z0 * 2 + 1 - y
            along_y(k, 0, 0, o).wait_recv()

    def product(k):
        @pl.loop(0, n_row)
        def _(j):
            if k == 0:
                acc[j] = blocks_product(k, j)
            else:
                acc[j] += blocks_product(k, j)

    for k in range(CHUNKS):
        post(k)
    forward(0, start, True)
    gram = None
    pieces = iter(range(S_COPIES))
    for k in range(CHUNKS - 1):
        for _ in range(2):
            convert(next(pieces))
        forward(k + 1, start, True)
        if k > 0:
            convert(next(pieces))
        if k == CHUNKS - 2:
            for piece in pieces:
                convert(piece)
        complete(k)
        gram = inner(k) if gram is None else gram + inner(k)
        product(k)

    last = CHUNKS - 1
    complete(last)
    cbuf[r] = gram + inner(last)

    def c_copy(p, q):
        return remote(cbuf.at[q], cbuf.at[q], c_send.at[p], c_recv.at[q], {"row": p, "col": c})

    others(n_row, r, lambda p: c_copy(p, r).start())

    def core_copy(i, j):
        return remote(acc.at[j], rbuf.at[i], core_send.at[i], core_recv.at[i],
                      {"row": near, "col": c})

    acc[cross] += blocks_product(last, cross)
    core_copy(0, cross).start()
    acc[near] += blocks_product(last, near)
    core_copy(1, near).start()

    others(n_row, r, lambda q: c_copy(q, q).wait_recv())
    total = cbuf[0]
    for q in range(1, n_row):
        total = total + cbuf[q]
    ab[c] = total

    def ab_copy(p, q):
        return remote(ab.at[q], ab.at[q], ab_send.at[p], ab_recv.at[q], {"row": r, "col": p})

    others(n_col, c, lambda p: ab_copy(p, c).start())

    acc[far] += blocks_product(last, far)
    core_copy(0, cross).wait_recv()
    xout[...] = (acc[far] + rbuf[0]).astype(jnp.bfloat16)
    x_copy = remote(xout, xbuf, x_send, x_recv, {"row": far, "col": c})
    x_copy.start()
    acc[r] += blocks_product(last, r)

    others(n_dev, me, lambda s: e_copy(s, s).wait_recv())
    for t, dest in ((0, xe), (1, ge)):
        turned = dot(perm[...], ebuf[:, t].reshape(n_out, LANES)).astype(jnp.bfloat16)
        for g in range(groups):
            dest[:, g * LANES:(g + 1) * LANES] = turned[g * wide:(g + 1) * wide]

    others(n_col, c, lambda q: ab_copy(q, q).wait_recv())
    orb_orb = ab[:, :tall, :].reshape(wide, wide)
    orb_grad = ab[:, tall:, :].reshape(wide, wide).T

    def accurate(left, right):
        high = left.astype(jnp.bfloat16)
        low = (left - high.astype(jnp.float32)).astype(jnp.bfloat16)
        return dot(high, right) + dot(low, right)

    rest = ge[...].astype(jnp.float32) - 0.5 * (
        accurate(orb_orb, ge[...]) + accurate(orb_grad, xe[...]))
    core_copy(1, near).wait_recv()
    rest = rest - (acc[r] + rbuf[1])
    x_copy.wait_recv()
    result = (rest - xbuf[...].astype(jnp.float32)).astype(jnp.bfloat16)
    stack = jnp.concatenate([result[:, g * LANES:(g + 1) * LANES] for g in range(groups)], axis=0)
    tiles = dot(back[...], stack)
    fbuf[...] = tiles.astype(jnp.bfloat16).reshape(n_dev, TILE, LANES)

    def f_copy(d, s):
        return remote(fbuf.at[d], out.at[s], f_send.at[d], f_recv.at[s], device(d))

    others(n_dev, me, lambda d: f_copy(d, me).start())
    out[me] = fbuf[me]

    others(n_row, r, lambda p: row_copy(p, r).wait_send())
    others(n_row, r, lambda p: c_copy(p, r).wait_send())
    others(n_col, c, lambda p: ab_copy(p, c).wait_send())
    others(n_dev, me, lambda d: e_copy(d, me).wait_send())
    for k in range(CHUNKS):
        spread(k, wait_send)
        forward(k, wait_send, False)
    core_copy(0, cross).wait_send()
    core_copy(1, near).wait_send()
    x_copy.wait_send()
    others(n_dev, me, lambda s: f_copy(s, s).wait_recv())
    others(n_dev, me, lambda d: f_copy(d, me).wait_send())


def kernel_body(n_row, n_col, orbitals, gradient, stored):
    own, n_orb = orbitals.shape
    n_dev = n_row * n_col
    width = n_orb // n_dev
    groups = width // LANES
    n_pw = own * n_dev
    tall = n_row * own
    deep = n_orb // n_row // CHUNKS

    def tiled(rows):
        shaped = rows.reshape(own, n_dev, groups, LANES)
        return shaped.transpose(1, 2, 0, 3).reshape(n_dev, TILE, LANES)

    def gather_rows(blocks, rows):
        perm = np.zeros((blocks * TILE, blocks * TILE), np.float32)
        for at in range(blocks * TILE):
            group, rest = divmod(at, blocks * rows)
            block, row = divmod(rest, rows)
            perm[at, block * TILE + group * rows + row] = 1.0
        return perm

    def by_lanes(perm):
        return jnp.asarray(perm.reshape(perm.shape[0], -1, LANES).transpose(1, 0, 2), jnp.bfloat16)

    perm = gather_rows(n_dev, own)
    small = jnp.asarray(gather_rows(n_row, own), jnp.bfloat16)
    bf16, f32 = jnp.bfloat16, jnp.float32
    dma = pltpu.SemaphoreType.DMA
    tiles = pl.pallas_call(
        functools.partial(kernel, n_row, n_col, own, width),
        out_shape=jax.ShapeDtypeStruct((n_dev, TILE, LANES), bf16),
        in_specs=[pl.BlockSpec(memory_space=pl.ANY)] * 6,
        out_specs=pl.BlockSpec(memory_space=pltpu.VMEM),
        scratch_shapes=[
            pltpu.VMEM((n_dev, 2, TILE, LANES), bf16),
            pltpu.VMEM((n_row * TILE, n_row * TILE), bf16),
            pltpu.VMEM((S_SLOTS, stored.shape[0] // S_COPIES, stored.shape[1]), f32),
            pltpu.VMEM(stored.shape, bf16),
            pltpu.VMEM((n_row, n_col, 2, TILE, LANES), bf16),
            pltpu.VMEM((CHUNKS, n_pw, deep), bf16),
            pltpu.VMEM((CHUNKS, 2 * tall, deep), bf16),
            pltpu.VMEM((n_row, n_pw, width), f32),
            pltpu.VMEM((2, n_pw, width), f32),
            pltpu.VMEM((n_pw, width), bf16),
            pltpu.VMEM((n_pw, width), bf16),
            pltpu.VMEM((n_dev, 2, TILE, LANES), bf16),
            pltpu.VMEM((n_pw, width), bf16),
            pltpu.VMEM((n_pw, width), bf16),
            pltpu.VMEM((n_dev * TILE, n_dev * TILE), bf16),
            pltpu.VMEM((n_dev * TILE, n_dev * TILE), bf16),
            pltpu.VMEM((n_row, 2 * tall, n_pw), f32),
            pltpu.VMEM((n_col, 2 * tall, n_pw), f32),
            pltpu.VMEM((n_dev, TILE, LANES), bf16),
            dma((3 + 2 * n_dev * TILE // LANES,)), dma((S_COPIES,)), dma((n_row,)), dma((n_row,)), dma((n_dev,)), dma((n_dev,)),
            dma((CHUNKS, 2, n_col // 2, 2)), dma((CHUNKS, n_col)),
            dma((n_row,)), dma((n_row,)), dma((n_col,)), dma((n_col,)),
            dma((2,)), dma((2,)), dma(()), dma(()), dma((n_dev,)), dma((n_dev,)),
        ],
        compiler_params=pltpu.CompilerParams(
            collective_id=0, has_side_effects=True, vmem_limit_bytes=56 * 1024 * 1024),
        cost_estimate=pl.CostEstimate(
            flops=2 * n_pw * stored.size, bytes_accessed=4 * stored.size, transcendentals=0),
    )(tiled(orbitals), tiled(gradient), by_lanes(perm), by_lanes(perm.T), small, stored)
    shaped = tiles.reshape(n_dev, groups, own, LANES)
    return shaped.transpose(2, 0, 1, 3).reshape(own, n_orb)


def body(orbitals, gradient, stored):
    n_row = lax.axis_size("row")
    n_col = lax.axis_size("col")
    own, n_orb = orbitals.shape
    n_dev = n_row * n_col
    width = n_orb // n_dev
    fits = (
        n_row == 4 and n_col % CHUNKS == 0 and width % LANES == 0
        and own * width == TILE * LANES and own * n_row == TILE
        and own * n_dev == LANES and stored.shape[0] % S_COPIES == 0
        and stored.size * 4 <= 32 * 1024 * 1024
    )
    if fits:
        return kernel_body(n_row, n_col, orbitals, gradient, stored)
    return general_body(orbitals, gradient, stored)


def solution(mesh):
    return jax.shard_map(
        body,
        mesh=mesh,
        in_specs=(P(("row", "col"), None), P(("row", "col"), None), P("row", "col")),
        out_specs=P(("row", "col"), None),
        check_vma=False,
    )
```

```python
import functools

import jax
import jax.numpy as jnp
import numpy as np
from jax import lax
from jax.experimental import pallas as pl
from jax.experimental.pallas import tpu as pltpu
from jax.sharding import PartitionSpec as P

MESH = pl.DeviceIdType.MESH
LANES = 128
TILE = 16
CHUNKS = 4
S_COPIES = 8
S_SLOTS = 6


def reorder(panel, outer, inner):
    width = panel.shape[1]
    shaped = panel.reshape(outer, inner, -1, width)
    return jnp.swapaxes(shaped, 0, 1).reshape(-1, width)


def inner_product(left, right):
    return lax.dot_general(
        left, right, (((0,), (0,)), ((), ())), preferred_element_type=jnp.float32
    )


def dot(left, right):
    return jnp.dot(left, right, preferred_element_type=jnp.float32)


def general_body(orbitals, gradient, stored):
    n_row = lax.axis_size("row")
    n_col = lax.axis_size("col")
    orb_q, grad_q = (
        lax.all_to_all(orbitals, "row", split_axis=1, concat_axis=0, tiled=True),
        lax.all_to_all(gradient, "row", split_axis=1, concat_axis=0, tiled=True),
    )
    orb_q, grad_q = (
        lax.all_gather(orb_q, "col", axis=0, tiled=True),
        lax.all_gather(grad_q, "col", axis=0, tiled=True),
    )
    orb_q = reorder(orb_q, n_col, n_row)
    grad_q = reorder(grad_q, n_col, n_row)
    orb_o, grad_o = (
        lax.all_to_all(orbitals, "col", split_axis=1, concat_axis=0, tiled=True),
        lax.all_to_all(gradient, "col", split_axis=1, concat_axis=0, tiled=True),
    )
    orb_o, grad_o = (
        lax.all_gather(orb_o, "row", axis=0, tiled=True),
        lax.all_gather(grad_o, "row", axis=0, tiled=True),
    )
    half = (0.5 * inner_product(orb_q, grad_o) + 0.5 * stored).astype(jnp.bfloat16)
    half_mirror = (0.5 * inner_product(grad_q, orb_o) + 0.5 * stored).astype(jnp.bfloat16)
    share = lax.psum_scatter(
        dot(orb_q, half) + dot(orb_q, half_mirror), "row", scatter_dimension=0, tiled=True
    )
    correction = lax.all_to_all(share, "col", split_axis=0, concat_axis=1, tiled=True)
    return (gradient.astype(jnp.float32) - correction).astype(jnp.bfloat16)


def kernel(
    n_row, n_col, own, width,
    x_hbm, g_hbm, perm_hbm, back_hbm, small_hbm, s_hbm, out,
    xg, small, sbuf, sb, rowbuf, xq, gsh, acc, rbuf, xout, xbuf, ebuf, xe, ge, perm, back, cbuf, ab, fbuf,
    in_sem, s_sem, row_send, row_recv, e_send, e_recv, g_send, g_recv,
    c_send, c_recv, ab_send, ab_recv, core_send, core_recv, x_send, x_recv, f_send, f_recv,
):
    n_dev = n_row * n_col
    n_z = n_col // 2
    groups = width // LANES
    part = n_col // CHUNKS
    deep = part * width
    r, c = lax.axis_index("row"), lax.axis_index("col")
    me = c * n_row + r
    z, y = lax.div(c, 2), lax.rem(c, 2)
    core, chip = lax.rem(r, 2), lax.div(r, 2)
    near = chip * 2 + 1 - core
    far = (1 - chip) * 2 + core
    cross = (1 - chip) * 2 + 1 - core

    def device(d):
        return {"row": lax.rem(d, n_row), "col": lax.div(d, n_row)}

    def remote(src, dst, send, recv, target):
        return pltpu.make_async_remote_copy(
            src_ref=src, dst_ref=dst, send_sem=send, recv_sem=recv,
            device_id=target, device_id_type=MESH,
        )

    depth = sbuf.shape[1]
    strip = 32

    def s_copy(i):
        return pltpu.make_async_copy(
            s_hbm.at[pl.ds(i * depth, depth), :], sbuf.at[i % S_SLOTS], s_sem.at[i])

    def convert(i):
        s_copy(i).wait()

        @pl.loop(0, depth // strip)
        def _(n):
            rows = pl.ds(pl.multiple_of(n * strip, strip), strip)
            into = pl.ds(pl.multiple_of(i * depth + n * strip, strip), strip)
            sb[into, :] = sbuf[i % S_SLOTS, rows, :].astype(jnp.bfloat16)

        if i + S_SLOTS < S_COPIES:
            s_copy(i + S_SLOTS).start()

    local = [
        pltpu.make_async_copy(x_hbm, xg.at[:, 0], in_sem.at[0]),
        pltpu.make_async_copy(g_hbm, xg.at[:, 1], in_sem.at[1]),
        pltpu.make_async_copy(small_hbm, small, in_sem.at[2]),
    ] + [
        pltpu.make_async_copy(
            perm_hbm.at[g], perm.at[:, pl.ds(g * LANES, LANES)], in_sem.at[3 + g])
        for g in range(perm_hbm.shape[0])
    ] + [
        pltpu.make_async_copy(
            back_hbm.at[g], back.at[:, pl.ds(g * LANES, LANES)],
            in_sem.at[3 + perm_hbm.shape[0] + g])
        for g in range(perm_hbm.shape[0])
    ]
    for copy in local:
        copy.start()
    for i in range(S_SLOTS):
        s_copy(i).start()

    def others(count, mine, body):
        @pl.loop(1, count)
        def _(i):
            body(lax.rem(mine + i, count))

    barrier = pltpu.get_barrier_semaphore()
    others(n_dev, me, lambda d: pl.semaphore_signal(
        barrier, inc=1, device_id=device(d), device_id_type=MESH))
    for copy in local:
        copy.wait()
    pl.semaphore_wait(barrier, n_dev - 1)

    def row_copy(p, q):
        return remote(
            xg.at[pl.ds(p * n_col, n_col)], rowbuf.at[q],
            row_send.at[p], row_recv.at[q], {"row": p, "col": c},
        )

    others(n_row, r, lambda p: row_copy(p, r).start())
    rowbuf[r] = xg[pl.ds(r * n_col, n_col)]

    def e_copy(d, s):
        return remote(xg.at[d], ebuf.at[s], e_send, e_recv, device(d))

    for i in range(S_COPIES // 2):
        convert(i)
    n_out = n_dev * TILE
    wide = n_dev * own
    tall = n_row * own
    others(n_row, r, lambda q: row_copy(q, q).wait_recv())

    def shard(k, o):
        return xq.at[k, pl.ds(pl.multiple_of(o * tall, tall), tall), :]

    def g_copy(k, o, send, target):
        return remote(
            shard(k, o), shard(k, o), send, g_recv.at[k, o], {"row": r, "col": target})

    def along_z(k, side, d):
        return g_copy(k, c, g_send.at[k, side, d, 0], c + 2 * d if side == 0 else c - 2 * d)

    def along_y(k, side, d, o):
        return g_copy(k, o, g_send.at[k, side, d, 1], z * 2 + 1 - y)

    def spread(k, do):
        do(along_y(k, 0, 0, c))
        for d in range(1, n_z):
            pl.when(z + d < n_z)(lambda d=d: do(along_z(k, 0, d)))
            pl.when(z >= d)(lambda d=d: do(along_z(k, 1, d)))

    def start(copy):
        copy.start()

    def wait_send(copy):
        copy.wait_send()

    def post(k):
        mine = pl.ds(pl.multiple_of(c * tall, tall), tall)
        for b in range(part):
            for t in range(2):
                block = rowbuf[:, k * part + b, t].reshape(n_row * TILE, LANES)
                turned = dot(small[...], block).astype(jnp.bfloat16)
                for g in range(groups):
                    piece = turned[g * tall:(g + 1) * tall]
                    lanes = pl.ds(b * width + g * LANES, LANES)
                    gsh[k, t * tall:(t + 1) * tall, lanes] = piece
                    if t == 0:
                        xq[k, mine, lanes] = piece
        spread(k, start)

    def forward(k, do, receive):
        def step(side, d, o):
            copy = along_y(k, side, d, o)
            if receive:
                copy.wait_recv()
            do(copy)

        for d in range(1, n_z):
            pl.when(z + d < n_z)(lambda d=d: step(0, d, c + 2 * d))
            pl.when(z >= d)(lambda d=d: step(1, d, c - 2 * d))

    def blocks_product(k, j):
        rows = pl.ds(k * deep, deep)
        cols = pl.ds(pl.multiple_of(j * width, width), width)
        return dot(xq[k], sb[rows, cols])

    def inner(k):
        return lax.dot_general(
            gsh[k], xq[k], (((1,), (1,)), ((), ())), preferred_element_type=jnp.float32)

    def complete(k):
        for z0 in range(n_z):
            o = z0 * 2 + 1 - y
            along_y(k, 0, 0, o).wait_recv()

    def product(k):
        @pl.loop(0, n_row)
        def _(j):
            if k == 0:
                acc[j] = blocks_product(k, j)
            else:
                acc[j] += blocks_product(k, j)

    for k in range(CHUNKS):
        post(k)
    gram = None
    for k in range(CHUNKS + 1):
        if k < CHUNKS:
            forward(k, start, True)
        if k == CHUNKS - 1:
            others(n_dev, me, lambda d: e_copy(d, me).start())
            ebuf[me] = xg[me]
        piece = S_COPIES // 2 + k
        if piece < S_COPIES:
            convert(piece)
        if 1 <= k < CHUNKS:
            complete(k - 1)
            gram = inner(k - 1) if gram is None else gram + inner(k - 1)
            product(k - 1)

    last = CHUNKS - 1
    complete(last)
    cbuf[r] = gram + inner(last)

    def c_copy(p, q):
        return remote(cbuf.at[q], cbuf.at[q], c_send.at[p], c_recv.at[q], {"row": p, "col": c})

    others(n_row, r, lambda p: c_copy(p, r).start())

    def core_copy(i, j):
        return remote(acc.at[j], rbuf.at[i], core_send.at[i], core_recv.at[i],
                      {"row": near, "col": c})

    acc[cross] += blocks_product(last, cross)
    core_copy(0, cross).start()
    acc[near] += blocks_product(last, near)
    core_copy(1, near).start()

    others(n_row, r, lambda q: c_copy(q, q).wait_recv())
    total = cbuf[0]
    for q in range(1, n_row):
        total = total + cbuf[q]
    ab[c] = total

    def ab_copy(p, q):
        return remote(ab.at[q], ab.at[q], ab_send.at[p], ab_recv.at[q], {"row": r, "col": p})

    others(n_col, c, lambda p: ab_copy(p, c).start())

    acc[far] += blocks_product(last, far)
    core_copy(0, cross).wait_recv()
    xout[...] = (acc[far] + rbuf[0]).astype(jnp.bfloat16)
    x_copy = remote(xout, xbuf, x_send, x_recv, {"row": far, "col": c})
    x_copy.start()
    acc[r] += blocks_product(last, r)

    rest_of = pl.ds(0, n_dev - 1)
    e_all = remote(xg.at[rest_of], ebuf.at[rest_of], e_send, e_recv, device(me))
    e_all.wait_recv()
    for t, dest in ((0, xe), (1, ge)):
        turned = dot(perm[...], ebuf[:, t].reshape(n_out, LANES)).astype(jnp.bfloat16)
        for g in range(groups):
            dest[:, g * LANES:(g + 1) * LANES] = turned[g * wide:(g + 1) * wide]

    others(n_col, c, lambda q: ab_copy(q, q).wait_recv())
    orb_orb = ab[:, :tall, :].reshape(wide, wide)
    orb_grad = ab[:, tall:, :].reshape(wide, wide).T

    def accurate(left, right):
        high = left.astype(jnp.bfloat16)
        low = (left - high.astype(jnp.float32)).astype(jnp.bfloat16)
        return dot(high, right) + dot(low, right)

    rest = ge[...].astype(jnp.float32) - 0.5 * (
        accurate(orb_orb, ge[...]) + accurate(orb_grad, xe[...]))
    core_copy(1, near).wait_recv()
    rest = rest - (acc[r] + rbuf[1])
    x_copy.wait_recv()
    result = (rest - xbuf[...].astype(jnp.float32)).astype(jnp.bfloat16)
    stack = jnp.concatenate([result[:, g * LANES:(g + 1) * LANES] for g in range(groups)], axis=0)
    tiles = dot(back[...], stack)
    fbuf[...] = tiles.astype(jnp.bfloat16).reshape(n_dev, TILE, LANES)

    def f_copy(d, s):
        return remote(fbuf.at[d], out.at[s], f_send, f_recv, device(d))

    others(n_dev, me, lambda d: f_copy(d, me).start())
    out[me] = fbuf[me]

    others(n_row, r, lambda p: row_copy(p, r).wait_send())
    others(n_row, r, lambda p: c_copy(p, r).wait_send())
    others(n_col, c, lambda p: ab_copy(p, c).wait_send())
    e_all.wait_send()
    for k in range(CHUNKS):
        spread(k, wait_send)
        forward(k, wait_send, False)
    core_copy(0, cross).wait_send()
    core_copy(1, near).wait_send()
    x_copy.wait_send()
    f_all = remote(fbuf.at[rest_of], out.at[rest_of], f_send, f_recv, device(me))
    f_all.wait_recv()
    f_all.wait_send()


def kernel_body(n_row, n_col, orbitals, gradient, stored):
    own, n_orb = orbitals.shape
    n_dev = n_row * n_col
    width = n_orb // n_dev
    groups = width // LANES
    n_pw = own * n_dev
    tall = n_row * own
    deep = n_orb // n_row // CHUNKS

    def tiled(rows):
        shaped = rows.reshape(own, n_dev, groups, LANES)
        return shaped.transpose(1, 2, 0, 3).reshape(n_dev, TILE, LANES)

    def gather_rows(blocks, rows):
        perm = np.zeros((blocks * TILE, blocks * TILE), np.float32)
        for at in range(blocks * TILE):
            group, rest = divmod(at, blocks * rows)
            block, row = divmod(rest, rows)
            perm[at, block * TILE + group * rows + row] = 1.0
        return perm

    def by_lanes(perm):
        return jnp.asarray(perm.reshape(perm.shape[0], -1, LANES).transpose(1, 0, 2), jnp.bfloat16)

    perm = gather_rows(n_dev, own)
    small = jnp.asarray(gather_rows(n_row, own), jnp.bfloat16)
    bf16, f32 = jnp.bfloat16, jnp.float32
    dma = pltpu.SemaphoreType.DMA
    tiles = pl.pallas_call(
        functools.partial(kernel, n_row, n_col, own, width),
        out_shape=jax.ShapeDtypeStruct((n_dev, TILE, LANES), bf16),
        in_specs=[pl.BlockSpec(memory_space=pl.ANY)] * 6,
        out_specs=pl.BlockSpec(memory_space=pltpu.VMEM),
        scratch_shapes=[
            pltpu.VMEM((n_dev, 2, TILE, LANES), bf16),
            pltpu.VMEM((n_row * TILE, n_row * TILE), bf16),
            pltpu.VMEM((S_SLOTS, stored.shape[0] // S_COPIES, stored.shape[1]), f32),
            pltpu.VMEM(stored.shape, bf16),
            pltpu.VMEM((n_row, n_col, 2, TILE, LANES), bf16),
            pltpu.VMEM((CHUNKS, n_pw, deep), bf16),
            pltpu.VMEM((CHUNKS, 2 * tall, deep), bf16),
            pltpu.VMEM((n_row, n_pw, width), f32),
            pltpu.VMEM((2, n_pw, width), f32),
            pltpu.VMEM((n_pw, width), bf16),
            pltpu.VMEM((n_pw, width), bf16),
            pltpu.VMEM((n_dev, 2, TILE, LANES), bf16),
            pltpu.VMEM((n_pw, width), bf16),
            pltpu.VMEM((n_pw, width), bf16),
            pltpu.VMEM((n_dev * TILE, n_dev * TILE), bf16),
            pltpu.VMEM((n_dev * TILE, n_dev * TILE), bf16),
            pltpu.VMEM((n_row, 2 * tall, n_pw), f32),
            pltpu.VMEM((n_col, 2 * tall, n_pw), f32),
            pltpu.VMEM((n_dev, TILE, LANES), bf16),
            dma((3 + 2 * n_dev * TILE // LANES,)), dma((S_COPIES,)), dma((n_row,)), dma((n_row,)), dma(()), dma(()),
            dma((CHUNKS, 2, n_col // 2, 2)), dma((CHUNKS, n_col)),
            dma((n_row,)), dma((n_row,)), dma((n_col,)), dma((n_col,)),
            dma((2,)), dma((2,)), dma(()), dma(()), dma(()), dma(()),
        ],
        compiler_params=pltpu.CompilerParams(
            collective_id=0, has_side_effects=True, vmem_limit_bytes=56 * 1024 * 1024),
        cost_estimate=pl.CostEstimate(
            flops=2 * n_pw * stored.size, bytes_accessed=4 * stored.size, transcendentals=0),
    )(tiled(orbitals), tiled(gradient), by_lanes(perm), by_lanes(perm.T), small, stored)
    shaped = tiles.reshape(n_dev, groups, own, LANES)
    return shaped.transpose(2, 0, 1, 3).reshape(own, n_orb)


def body(orbitals, gradient, stored):
    n_row = lax.axis_size("row")
    n_col = lax.axis_size("col")
    own, n_orb = orbitals.shape
    n_dev = n_row * n_col
    width = n_orb // n_dev
    fits = (
        n_row == 4 and n_col % CHUNKS == 0 and width % LANES == 0
        and own * width == TILE * LANES and own * n_row == TILE
        and own * n_dev == LANES and stored.shape[0] % S_COPIES == 0
        and stored.size * 4 <= 32 * 1024 * 1024
    )
    if fits:
        return kernel_body(n_row, n_col, orbitals, gradient, stored)
    return general_body(orbitals, gradient, stored)


def solution(mesh):
    return jax.shard_map(
        body,
        mesh=mesh,
        in_specs=(P(("row", "col"), None), P(("row", "col"), None), P("row", "col")),
        out_specs=P(("row", "col"), None),
        check_vma=False,
    )
```

```python
import functools

import jax
import jax.numpy as jnp
import numpy as np
from jax import lax
from jax.experimental import pallas as pl
from jax.experimental.pallas import tpu as pltpu
from jax.sharding import PartitionSpec as P

MESH = pl.DeviceIdType.MESH
LANES = 128
TILE = 16
CHUNKS = 8
S_COPIES = 8
S_SLOTS = 6


def reorder(panel, outer, inner):
    width = panel.shape[1]
    shaped = panel.reshape(outer, inner, -1, width)
    return jnp.swapaxes(shaped, 0, 1).reshape(-1, width)


def inner_product(left, right):
    return lax.dot_general(
        left, right, (((0,), (0,)), ((), ())), preferred_element_type=jnp.float32
    )


def dot(left, right):
    return jnp.dot(left, right, preferred_element_type=jnp.float32)


def general_body(orbitals, gradient, stored):
    n_row = lax.axis_size("row")
    n_col = lax.axis_size("col")
    orb_q, grad_q = (
        lax.all_to_all(orbitals, "row", split_axis=1, concat_axis=0, tiled=True),
        lax.all_to_all(gradient, "row", split_axis=1, concat_axis=0, tiled=True),
    )
    orb_q, grad_q = (
        lax.all_gather(orb_q, "col", axis=0, tiled=True),
        lax.all_gather(grad_q, "col", axis=0, tiled=True),
    )
    orb_q = reorder(orb_q, n_col, n_row)
    grad_q = reorder(grad_q, n_col, n_row)
    orb_o, grad_o = (
        lax.all_to_all(orbitals, "col", split_axis=1, concat_axis=0, tiled=True),
        lax.all_to_all(gradient, "col", split_axis=1, concat_axis=0, tiled=True),
    )
    orb_o, grad_o = (
        lax.all_gather(orb_o, "row", axis=0, tiled=True),
        lax.all_gather(grad_o, "row", axis=0, tiled=True),
    )
    half = (0.5 * inner_product(orb_q, grad_o) + 0.5 * stored).astype(jnp.bfloat16)
    half_mirror = (0.5 * inner_product(grad_q, orb_o) + 0.5 * stored).astype(jnp.bfloat16)
    share = lax.psum_scatter(
        dot(orb_q, half) + dot(orb_q, half_mirror), "row", scatter_dimension=0, tiled=True
    )
    correction = lax.all_to_all(share, "col", split_axis=0, concat_axis=1, tiled=True)
    return (gradient.astype(jnp.float32) - correction).astype(jnp.bfloat16)


def kernel(
    n_row, n_col, own, width,
    x_hbm, g_hbm, perm_hbm, back_hbm, small_hbm, s_hbm, out,
    xg, small, sbuf, sb, rowbuf, xq, gsh, acc, rbuf, xout, xbuf, ebuf, xe, ge, perm, back, cbuf, ab, fbuf,
    in_sem, s_sem, row_send, row_recv, e_send, e_recv, g_send, g_recv,
    c_send, c_recv, ab_send, ab_recv, core_send, core_recv, x_send, x_recv, f_send, f_recv,
):
    n_dev = n_row * n_col
    n_z = n_col // 2
    groups = width // LANES
    part = n_col // CHUNKS
    deep = part * width
    r, c = lax.axis_index("row"), lax.axis_index("col")
    me = c * n_row + r
    z, y = lax.div(c, 2), lax.rem(c, 2)
    core, chip = lax.rem(r, 2), lax.div(r, 2)
    near = chip * 2 + 1 - core
    far = (1 - chip) * 2 + core
    cross = (1 - chip) * 2 + 1 - core

    def device(d):
        return {"row": lax.rem(d, n_row), "col": lax.div(d, n_row)}

    def remote(src, dst, send, recv, target):
        return pltpu.make_async_remote_copy(
            src_ref=src, dst_ref=dst, send_sem=send, recv_sem=recv,
            device_id=target, device_id_type=MESH,
        )

    depth = sbuf.shape[1]
    strip = 32

    def s_copy(i):
        return pltpu.make_async_copy(
            s_hbm.at[pl.ds(i * depth, depth), :], sbuf.at[i % S_SLOTS], s_sem.at[i])

    def convert(i):
        s_copy(i).wait()

        @pl.loop(0, depth // strip)
        def _(n):
            rows = pl.ds(pl.multiple_of(n * strip, strip), strip)
            into = pl.ds(pl.multiple_of(i * depth + n * strip, strip), strip)
            sb[into, :] = sbuf[i % S_SLOTS, rows, :].astype(jnp.bfloat16)

        if i + S_SLOTS < S_COPIES:
            s_copy(i + S_SLOTS).start()

    local = [
        pltpu.make_async_copy(x_hbm, xg.at[:, 0], in_sem.at[0]),
        pltpu.make_async_copy(g_hbm, xg.at[:, 1], in_sem.at[1]),
        pltpu.make_async_copy(small_hbm, small, in_sem.at[2]),
    ] + [
        pltpu.make_async_copy(
            perm_hbm.at[g], perm.at[:, pl.ds(g * LANES, LANES)], in_sem.at[3 + g])
        for g in range(perm_hbm.shape[0])
    ] + [
        pltpu.make_async_copy(
            back_hbm.at[g], back.at[:, pl.ds(g * LANES, LANES)],
            in_sem.at[3 + perm_hbm.shape[0] + g])
        for g in range(perm_hbm.shape[0])
    ]
    for copy in local:
        copy.start()
    for i in range(S_SLOTS):
        s_copy(i).start()

    def others(count, mine, body):
        @pl.loop(1, count)
        def _(i):
            body(lax.rem(mine + i, count))

    barrier = pltpu.get_barrier_semaphore()
    others(n_dev, me, lambda d: pl.semaphore_signal(
        barrier, inc=1, device_id=device(d), device_id_type=MESH))
    for copy in local:
        copy.wait()
    pl.semaphore_wait(barrier, n_dev - 1)

    def row_copy(p, q):
        return remote(
            xg.at[pl.ds(p * n_col, n_col)], rowbuf.at[q],
            row_send.at[p], row_recv.at[q], {"row": p, "col": c},
        )

    others(n_row, r, lambda p: row_copy(p, r).start())
    rowbuf[r] = xg[pl.ds(r * n_col, n_col)]

    def e_copy(d, s):
        return remote(xg.at[d], ebuf.at[s], e_send, e_recv, device(d))

    for i in range(S_COPIES // 2):
        convert(i)
    n_out = n_dev * TILE
    wide = n_dev * own
    tall = n_row * own
    others(n_row, r, lambda q: row_copy(q, q).wait_recv())

    def shard(k, o):
        return xq.at[k, pl.ds(pl.multiple_of(o * tall, tall), tall), :]

    def g_copy(k, o, send, target):
        return remote(
            shard(k, o), shard(k, o), send, g_recv.at[k, o], {"row": r, "col": target})

    def along_z(k, side, d):
        return g_copy(k, c, g_send.at[k, side, d, 0], c + 2 * d if side == 0 else c - 2 * d)

    def along_y(k, side, d, o):
        return g_copy(k, o, g_send.at[k, side, d, 1], z * 2 + 1 - y)

    def spread(k, do):
        do(along_y(k, 0, 0, c))
        for d in range(1, n_z):
            pl.when(z + d < n_z)(lambda d=d: do(along_z(k, 0, d)))
            pl.when(z >= d)(lambda d=d: do(along_z(k, 1, d)))

    def start(copy):
        copy.start()

    def wait_send(copy):
        copy.wait_send()

    def post(k):
        mine = pl.ds(pl.multiple_of(c * tall, tall), tall)
        for b in range(part):
            for t in range(2):
                block = rowbuf[:, k * part + b, t].reshape(n_row * TILE, LANES)
                turned = dot(small[...], block).astype(jnp.bfloat16)
                for g in range(groups):
                    piece = turned[g * tall:(g + 1) * tall]
                    lanes = pl.ds(b * width + g * LANES, LANES)
                    gsh[k, t * tall:(t + 1) * tall, lanes] = piece
                    if t == 0:
                        xq[k, mine, lanes] = piece
        spread(k, start)

    def forward(k, do, receive):
        def step(side, d, o):
            copy = along_y(k, side, d, o)
            if receive:
                copy.wait_recv()
            do(copy)

        for d in range(1, n_z):
            pl.when(z + d < n_z)(lambda d=d: step(0, d, c + 2 * d))
            pl.when(z >= d)(lambda d=d: step(1, d, c - 2 * d))

    def blocks_product(k, j):
        rows = pl.ds(k * deep, deep)
        cols = pl.ds(pl.multiple_of(j * width, width), width)
        return dot(xq[k], sb[rows, cols])

    def inner(k):
        return lax.dot_general(
            gsh[k], xq[k], (((1,), (1,)), ((), ())), preferred_element_type=jnp.float32)

    def complete(k):
        for z0 in range(n_z):
            o = z0 * 2 + 1 - y
            along_y(k, 0, 0, o).wait_recv()

    def product(k):
        @pl.loop(0, n_row)
        def _(j):
            if k == 0:
                acc[j] = blocks_product(k, j)
            else:
                acc[j] += blocks_product(k, j)

    for k in range(CHUNKS):
        post(k)
    gram = None
    for k in range(CHUNKS + 1):
        if k < CHUNKS:
            forward(k, start, True)
        if k == CHUNKS - 1:
            others(n_dev, me, lambda d: e_copy(d, me).start())
            ebuf[me] = xg[me]
        piece = S_COPIES // 2 + k
        if piece < S_COPIES:
            convert(piece)
        if 1 <= k < CHUNKS:
            complete(k - 1)
            gram = inner(k - 1) if gram is None else gram + inner(k - 1)
            product(k - 1)

    last = CHUNKS - 1
    complete(last)
    cbuf[r] = gram + inner(last)

    def c_copy(p, q):
        return remote(cbuf.at[q], cbuf.at[q], c_send.at[p], c_recv.at[q], {"row": p, "col": c})

    others(n_row, r, lambda p: c_copy(p, r).start())

    def core_copy(i, j):
        return remote(acc.at[j], rbuf.at[i], core_send.at[i], core_recv.at[i],
                      {"row": near, "col": c})

    acc[cross] += blocks_product(last, cross)
    core_copy(0, cross).start()
    acc[near] += blocks_product(last, near)
    core_copy(1, near).start()

    others(n_row, r, lambda q: c_copy(q, q).wait_recv())
    total = cbuf[0]
    for q in range(1, n_row):
        total = total + cbuf[q]
    ab[c] = total

    def ab_copy(p, q):
        return remote(ab.at[q], ab.at[q], ab_send.at[p], ab_recv.at[q], {"row": r, "col": p})

    others(n_col, c, lambda p: ab_copy(p, c).start())

    acc[far] += blocks_product(last, far)
    core_copy(0, cross).wait_recv()
    xout[...] = (acc[far] + rbuf[0]).astype(jnp.bfloat16)
    x_copy = remote(xout, xbuf, x_send, x_recv, {"row": far, "col": c})
    x_copy.start()
    acc[r] += blocks_product(last, r)

    rest_of = pl.ds(0, n_dev - 1)
    e_all = remote(xg.at[rest_of], ebuf.at[rest_of], e_send, e_recv, device(me))
    e_all.wait_recv()
    for t, dest in ((0, xe), (1, ge)):
        turned = dot(perm[...], ebuf[:, t].reshape(n_out, LANES)).astype(jnp.bfloat16)
        for g in range(groups):
            dest[:, g * LANES:(g + 1) * LANES] = turned[g * wide:(g + 1) * wide]

    others(n_col, c, lambda q: ab_copy(q, q).wait_recv())
    orb_orb = ab[:, :tall, :].reshape(wide, wide)
    orb_grad = ab[:, tall:, :].reshape(wide, wide).T

    def accurate(left, right):
        high = left.astype(jnp.bfloat16)
        low = (left - high.astype(jnp.float32)).astype(jnp.bfloat16)
        return dot(high, right) + dot(low, right)

    rest = ge[...].astype(jnp.float32) - 0.5 * (
        accurate(orb_orb, ge[...]) + accurate(orb_grad, xe[...]))
    core_copy(1, near).wait_recv()
    rest = rest - (acc[r] + rbuf[1])
    x_copy.wait_recv()
    result = (rest - xbuf[...].astype(jnp.float32)).astype(jnp.bfloat16)
    stack = jnp.concatenate([result[:, g * LANES:(g + 1) * LANES] for g in range(groups)], axis=0)
    tiles = dot(back[...], stack)
    fbuf[...] = tiles.astype(jnp.bfloat16).reshape(n_dev, TILE, LANES)

    def f_copy(d, s):
        return remote(fbuf.at[d], out.at[s], f_send, f_recv, device(d))

    others(n_dev, me, lambda d: f_copy(d, me).start())
    out[me] = fbuf[me]

    others(n_row, r, lambda p: row_copy(p, r).wait_send())
    others(n_row, r, lambda p: c_copy(p, r).wait_send())
    others(n_col, c, lambda p: ab_copy(p, c).wait_send())
    e_all.wait_send()
    for k in range(CHUNKS):
        spread(k, wait_send)
        forward(k, wait_send, False)
    core_copy(0, cross).wait_send()
    core_copy(1, near).wait_send()
    x_copy.wait_send()
    f_all = remote(fbuf.at[rest_of], out.at[rest_of], f_send, f_recv, device(me))
    f_all.wait_recv()
    f_all.wait_send()


def kernel_body(n_row, n_col, orbitals, gradient, stored):
    own, n_orb = orbitals.shape
    n_dev = n_row * n_col
    width = n_orb // n_dev
    groups = width // LANES
    n_pw = own * n_dev
    tall = n_row * own
    deep = n_orb // n_row // CHUNKS

    def tiled(rows):
        shaped = rows.reshape(own, n_dev, groups, LANES)
        return shaped.transpose(1, 2, 0, 3).reshape(n_dev, TILE, LANES)

    def gather_rows(blocks, rows):
        perm = np.zeros((blocks * TILE, blocks * TILE), np.float32)
        for at in range(blocks * TILE):
            group, rest = divmod(at, blocks * rows)
            block, row = divmod(rest, rows)
            perm[at, block * TILE + group * rows + row] = 1.0
        return perm

    def by_lanes(perm):
        return jnp.asarray(perm.reshape(perm.shape[0], -1, LANES).transpose(1, 0, 2), jnp.bfloat16)

    perm = gather_rows(n_dev, own)
    small = jnp.asarray(gather_rows(n_row, own), jnp.bfloat16)
    bf16, f32 = jnp.bfloat16, jnp.float32
    dma = pltpu.SemaphoreType.DMA
    tiles = pl.pallas_call(
        functools.partial(kernel, n_row, n_col, own, width),
        out_shape=jax.ShapeDtypeStruct((n_dev, TILE, LANES), bf16),
        in_specs=[pl.BlockSpec(memory_space=pl.ANY)] * 6,
        out_specs=pl.BlockSpec(memory_space=pltpu.VMEM),
        scratch_shapes=[
            pltpu.VMEM((n_dev, 2, TILE, LANES), bf16),
            pltpu.VMEM((n_row * TILE, n_row * TILE), bf16),
            pltpu.VMEM((S_SLOTS, stored.shape[0] // S_COPIES, stored.shape[1]), f32),
            pltpu.VMEM(stored.shape, bf16),
            pltpu.VMEM((n_row, n_col, 2, TILE, LANES), bf16),
            pltpu.VMEM((CHUNKS, n_pw, deep), bf16),
            pltpu.VMEM((CHUNKS, 2 * tall, deep), bf16),
            pltpu.VMEM((n_row, n_pw, width), f32),
            pltpu.VMEM((2, n_pw, width), f32),
            pltpu.VMEM((n_pw, width), bf16),
            pltpu.VMEM((n_pw, width), bf16),
            pltpu.VMEM((n_dev, 2, TILE, LANES), bf16),
            pltpu.VMEM((n_pw, width), bf16),
            pltpu.VMEM((n_pw, width), bf16),
            pltpu.VMEM((n_dev * TILE, n_dev * TILE), bf16),
            pltpu.VMEM((n_dev * TILE, n_dev * TILE), bf16),
            pltpu.VMEM((n_row, 2 * tall, n_pw), f32),
            pltpu.VMEM((n_col, 2 * tall, n_pw), f32),
            pltpu.VMEM((n_dev, TILE, LANES), bf16),
            dma((3 + 2 * n_dev * TILE // LANES,)), dma((S_COPIES,)), dma((n_row,)), dma((n_row,)), dma(()), dma(()),
            dma((CHUNKS, 2, n_col // 2, 2)), dma((CHUNKS, n_col)),
            dma((n_row,)), dma((n_row,)), dma((n_col,)), dma((n_col,)),
            dma((2,)), dma((2,)), dma(()), dma(()), dma(()), dma(()),
        ],
        compiler_params=pltpu.CompilerParams(
            collective_id=0, has_side_effects=True, vmem_limit_bytes=56 * 1024 * 1024),
        cost_estimate=pl.CostEstimate(
            flops=2 * n_pw * stored.size, bytes_accessed=4 * stored.size, transcendentals=0),
    )(tiled(orbitals), tiled(gradient), by_lanes(perm), by_lanes(perm.T), small, stored)
    shaped = tiles.reshape(n_dev, groups, own, LANES)
    return shaped.transpose(2, 0, 1, 3).reshape(own, n_orb)


def body(orbitals, gradient, stored):
    n_row = lax.axis_size("row")
    n_col = lax.axis_size("col")
    own, n_orb = orbitals.shape
    n_dev = n_row * n_col
    width = n_orb // n_dev
    fits = (
        n_row == 4 and n_col % CHUNKS == 0 and width % LANES == 0
        and own * width == TILE * LANES and own * n_row == TILE
        and own * n_dev == LANES and stored.shape[0] % S_COPIES == 0
        and stored.size * 4 <= 32 * 1024 * 1024
    )
    if fits:
        return kernel_body(n_row, n_col, orbitals, gradient, stored)
    return general_body(orbitals, gradient, stored)


def solution(mesh):
    return jax.shard_map(
        body,
        mesh=mesh,
        in_specs=(P(("row", "col"), None), P(("row", "col"), None), P("row", "col")),
        out_specs=P(("row", "col"), None),
        check_vma=False,
    )
```
